256 devices in a mesh: group: 16 (over y, z_lo, core), tensor: 16 (over z_hi, x).
Axes of the slice: x: 4, y: 4, z: 8 (z_hi: 4, z_lo: 2; z = z_hi * 2 + z_lo), core: 2. Of those that a mesh axis runs over, the one named last changes fastest.
Arguments:
- queries: bfloat16 [2048, 8192], P('group', 'tensor'), may hold values from -70 to 70
- keys_new: bfloat16 [2048, 2048], P('group', 'tensor'), may hold values from -6 to 6, as said below
- values_new: bfloat16 [2048, 2048], P('group', 'tensor'), may hold values from -6 to 6, as said below
- cache_keys: bfloat16 [64, 16, 512, 128], P('group', 'tensor'), may hold values from -6 to 6, as said below
- cache_values: bfloat16 [64, 16, 512, 128], P('group', 'tensor'), may hold values from -6 to 6, as said below
- cache_len: int32 [64], P('group'), may hold values from 128 to 512, as said below
- accepted: int32 [64], P('group'), may hold values from 1 to 32, as said below
- entering: bfloat16 [2048, 8192], P('group', 'tensor'), may hold values from -6 to 6
- low_feature: bfloat16 [2048, 8192], P('group', 'tensor'), may hold values from -6 to 6
- mid_feature: bfloat16 [2048, 8192], P('group', 'tensor'), may hold values from -6 to 6
- out_proj: bfloat16 [8192, 8192], P('tensor'), may hold values from -0.0625 to 0.0625
- join_weight: bfloat16 [3, 8192, 4096], P(None, 'tensor', 'group'), may hold values from -0.0390625 to 0.0390625
- teacher: bfloat16 [2048, 4096], P('group'), may hold values from -6 to 6
Outputs:
- high_feature: bfloat16 [2048, 8192], P('group', 'tensor')
- draft_grad: float32 [3, 8192, 4096], P(None, 'tensor', 'group')
The draws below stay inside these ranges and needn't reach their ends.
Inputs may be any that keep to these rules, and one draw needn't show every extreme that they name: `cache_len`: the first sequence of every group fills all 512 slots. `accepted`: the last sequence accepts all 32 tokens. `cache_keys`: entries t and u of the second dimension are equal where t * 8 // 16 equals u * 8 // 16. `cache_values`: entries t and u of the second dimension are equal where t * 8 // 16 equals u * 8 // 16. `keys_new`: column blocks t and u of 128 columns are equal where t * 8 // 16 equals u * 8 // 16. `values_new`: column blocks t and u of 128 columns are equal where t * 8 // 16 equals u * 8 // 16.
All inputs are finite; a program needn't handle non-finite values.
Results may differ from the reference program's by a relative error of at most 0.0065.
Values may be sent and summed in bfloat16 or wider, within the bound.
A program may use at most 128 MiB of HBM per device.

```python
import jax
import jax.numpy as jnp
from jax import lax

D = 8192
HD = 128
KVH = 8
H_DEV = 4
DF = 4096
POS = 32
SEQ_DEV = 4
L = 512
HEADS = 64
KV_HELD = 16
SEQ_ALL = 64
TOKENS = 2048
N_GROUP = 16


def spread_heads(values, axis):
    return jnp.repeat(values, KV_HELD // KVH, axis=axis)


def draw_queries(key, part):
    key = jax.random.fold_in(key, 11)
    return jnp.clip(jax.random.normal(key, (TOKENS, HEADS * HD), jnp.float32), -6.0, 6.0).astype(jnp.bfloat16)


def draw_cache_keys(key, part):
    key = jax.random.fold_in(key, 12)
    return spread_heads(jnp.clip(jax.random.normal(key, (SEQ_ALL, KVH, L, HD), jnp.float32), -6.0, 6.0), 1).astype(jnp.bfloat16)


def draw_cache_values(key, part):
    key = jax.random.fold_in(key, 15)
    return spread_heads(jnp.clip(jax.random.normal(key, (SEQ_ALL, KVH, L, HD), jnp.float32), -6.0, 6.0), 1).astype(jnp.bfloat16)


def draw_keys_new(key, part):
    key = jax.random.fold_in(key, 16)
    base = jnp.clip(jax.random.normal(key, (TOKENS, KVH, HD), jnp.float32), -6.0, 6.0)
    return spread_heads(base, 1).reshape(TOKENS, KV_HELD * HD).astype(jnp.bfloat16)


def draw_values_new(key, part):
    key = jax.random.fold_in(key, 17)
    base = jnp.clip(jax.random.normal(key, (TOKENS, KVH, HD), jnp.float32), -6.0, 6.0)
    return spread_heads(base, 1).reshape(TOKENS, KV_HELD * HD).astype(jnp.bfloat16)


def draw_cache_len(key, part):
    key = jax.random.fold_in(key, 13)
    drawn = jax.random.randint(key, (SEQ_ALL,), L // 4, L + 1)
    first = jnp.arange(SEQ_ALL) % SEQ_DEV == 0
    return jnp.where(first, L, drawn).astype(jnp.int32)


def draw_accepted(key, part):
    key = jax.random.fold_in(key, 14)
    groups = SEQ_ALL // SEQ_DEV
    index = jnp.arange(SEQ_ALL)
    rank = index // SEQ_DEV
    ceiling = POS // 4 + POS // 2 * rank // max(groups - 1, 1)
    drawn = jax.random.randint(key, (SEQ_ALL,), 1, ceiling + 1)
    return jnp.where(index == SEQ_ALL - 1, POS, drawn).astype(jnp.int32)


def level_of(stream_key, extent, split, low, high):
    loudness = 1.0
    for axis_at, blocks in split:
        heights = jax.random.uniform(jax.random.fold_in(jax.random.fold_in(stream_key, 6), axis_at), (blocks,), jnp.float32, low / len(split), high / len(split))
        loudness = loudness * jnp.repeat(jnp.exp(heights), extent[axis_at] // blocks).reshape((-1,) + (1,) * (len(extent) - 1 - axis_at))
    return loudness


def scatter_about(own_key, extent, deviation, most, shards=(), held_as=jnp.bfloat16):
    level = level_of(own_key, extent, shards, -0.22, 0.18) if shards else 1.0
    values = jax.random.normal(own_key, extent, jnp.float32) * deviation * level
    return jnp.minimum(jnp.maximum(values, -most), most).astype(held_as)


def setup_inputs(seed: int = 0) -> dict:
    streams_of = jax.random.split(jax.random.key(seed), 14)
    queries = draw_queries(jax.random.fold_in(streams_of[13], 71), 0)
    keys_new = draw_keys_new(jax.random.fold_in(streams_of[13], 71), 0)
    values_new = draw_values_new(jax.random.fold_in(streams_of[13], 71), 0)
    cache_keys = draw_cache_keys(jax.random.fold_in(streams_of[13], 71), 0)
    cache_values = draw_cache_values(jax.random.fold_in(streams_of[13], 71), 0)
    cache_len = draw_cache_len(jax.random.fold_in(streams_of[13], 71), 0)
    accepted = draw_accepted(jax.random.fold_in(streams_of[13], 71), 0)
    entering = scatter_about(streams_of[7], (TOKENS, D), 1.0, 6.0, ((0, 16), (1, 16)))
    low_feature = scatter_about(streams_of[8], (TOKENS, D), 1.0, 6.0, ((0, 16), (1, 16)))
    mid_feature = scatter_about(streams_of[9], (TOKENS, D), 1.0, 6.0, ((0, 16), (1, 16)))
    out_proj = scatter_about(streams_of[10], (HEADS * HD, D), (HEADS * HD) ** -0.5, 0.0625, ((0, 16),))
    join_weight = scatter_about(streams_of[11], (3, D, DF), (3 * D) ** -0.5, 0.0390625, ((1, 16), (2, 16)))
    teacher = scatter_about(streams_of[12], (TOKENS, DF), 1.0, 6.0, ((0, 16),))
    return dict(queries=queries, keys_new=keys_new, values_new=values_new, cache_keys=cache_keys, cache_values=cache_values, cache_len=cache_len, accepted=accepted, entering=entering, low_feature=low_feature, mid_feature=mid_feature, out_proj=out_proj, join_weight=join_weight, teacher=teacher)


def attend(query, key_new, value_new, cache_keys, cache_values, cache_len):
    scale = query.shape[-1] ** -0.5
    query_f = query.astype(jnp.float32)
    s_cache = jnp.einsum("spkhe,skle->skhpl", query_f, cache_keys.astype(jnp.float32)) * scale
    s_new = jnp.einsum("spkhe,sqke->skhpq", query_f, key_new.astype(jnp.float32)) * scale
    slots = jnp.arange(cache_keys.shape[2], dtype=jnp.int32)
    filled = slots[None, :] < cache_len[:, None]
    s_cache = jnp.where(filled[:, None, None, None, :], s_cache, -jnp.inf)
    places = jnp.arange(query.shape[1], dtype=jnp.int32)
    causal = places[None, :] <= places[:, None]
    s_new = jnp.where(causal, s_new, -jnp.inf)
    top = jnp.maximum(jnp.max(s_cache, axis=-1), jnp.max(s_new, axis=-1))
    p_cache = jnp.exp(s_cache - top[..., None])
    p_new = jnp.exp(s_new - top[..., None])
    total = jnp.sum(p_cache, axis=-1) + jnp.sum(p_new, axis=-1)
    w_cache = p_cache.astype(jnp.bfloat16).astype(jnp.float32)
    w_new = p_new.astype(jnp.bfloat16).astype(jnp.float32)
    mixed = jnp.einsum("skhpl,skle->skhpe", w_cache, cache_values.astype(jnp.float32))
    mixed = mixed + jnp.einsum("skhpq,sqke->skhpe", w_new, value_new.astype(jnp.float32))
    result = (mixed / total[..., None]).astype(jnp.bfloat16)
    return result.transpose(0, 3, 1, 2, 4)


def reference(queries, keys_new, values_new, cache_keys, cache_values, cache_len, accepted, entering, low_feature, mid_feature, out_proj, join_weight, teacher):
    query_g = queries.reshape(N_GROUP, SEQ_DEV, POS, KV_HELD, H_DEV, HD)
    key_g = keys_new.reshape(N_GROUP, SEQ_DEV, POS, KV_HELD, HD)
    value_g = values_new.reshape(N_GROUP, SEQ_DEV, POS, KV_HELD, HD)
    ckey_g = cache_keys.reshape(N_GROUP, SEQ_DEV, KV_HELD, L, HD)
    cval_g = cache_values.reshape(N_GROUP, SEQ_DEV, KV_HELD, L, HD)
    clen_g = cache_len.reshape(N_GROUP, SEQ_DEV)
    attended = lax.map(lambda a: attend(*a), (query_g, key_g, value_g, ckey_g, cval_g, clen_g))
    attended = attended.reshape(TOKENS, HEADS * HD)
    projected = jnp.dot(attended, out_proj, preferred_element_type=jnp.float32)
    high_feature = (entering.astype(jnp.float32) + projected).astype(jnp.bfloat16)
    features = jnp.stack([low_feature, mid_feature, high_feature], axis=1).reshape(TOKENS, 3 * D)
    joined = jnp.dot(features, join_weight.reshape(3 * D, DF), preferred_element_type=jnp.float32)
    place = jnp.arange(TOKENS, dtype=jnp.int32) % POS
    live = place < jnp.repeat(accepted, POS)
    group_total = jnp.sum(accepted.reshape(N_GROUP, SEQ_DEV).astype(jnp.float32), axis=1)
    row_scale = jnp.repeat(SEQ_DEV / group_total, SEQ_DEV * POS)
    error = (joined - teacher.astype(jnp.float32)) * row_scale[:, None]
    error = jnp.where(live[:, None], error, jnp.zeros_like(error)).astype(jnp.bfloat16)
    draft_grad = jnp.dot(features.T, error, preferred_element_type=jnp.float32).reshape(3, D, DF)
    return high_feature, draft_grad
```

```python
import jax
import jax.numpy as jnp
from jax import lax
from jax.experimental import pallas as pl
from jax.experimental.pallas import tpu as pltpu
from jax.sharding import PartitionSpec as P

MESH = pl.DeviceIdType.MESH
F32 = jnp.float32
BF16 = jnp.bfloat16
COPIES = 160
LOADS = 96
OTHER = {1: 3, 3: 1}


def xor4(v, k):
    return ((v // 2 + k // 2) % 2) * 2 + (v % 2 + k % 2) % 2


def dot(a, b):
    return jnp.dot(a, b, preferred_element_type=F32)


def dot_nt(a, b):
    return lax.dot_general(a, b, (((1,), (1,)), ((), ())), preferred_element_type=F32)


class Part:
    def __init__(self, bufs, x_first, a, a2):
        self.s1, self.r1, self.k1, self.s2, self.r2, self.k2, self.s3, self.r3, self.s4, self.r4 = bufs
        self.x_first, self.a, self.b, self.a2, self.b2 = x_first, a, OTHER[a], a2, OTHER[a2]
        self.order1 = (0, self.b, a, 2)
        self.order2 = (0, self.b2, a2, 2)

    def place(self, kz, kx):
        first, second = (kx, kz) if self.x_first else (kz, kx)
        return self.order1.index(first), self.order2.index(second)

    def store(self, kz, kx, columns, value):
        first, second = self.place(kz, kx)
        if first >= 2:
            self.s1[first - 2, second, :, columns] = value.astype(BF16)
        else:
            self.k1[first, second, :, columns] = value


def part_shapes(rows, width):
    return [
        pltpu.VMEM((2, 4, rows, width), BF16),
        pltpu.VMEM((2, 4, rows, width), BF16),
        pltpu.VMEM((2, 4, rows, width), F32),
        pltpu.VMEM((4, rows, width), BF16),
        pltpu.VMEM((4, rows, width), BF16),
        pltpu.VMEM((2, rows, width), F32),
        pltpu.VMEM((2, rows, width), BF16),
        pltpu.VMEM((2, rows, width), BF16),
        pltpu.VMEM((rows, width), BF16),
        pltpu.VMEM((rows, width), BF16),
    ]


PARTS = ((True, 1, 1), (True, 3, 3), (False, 1, 1), (False, 3, 3))
ROW_PARTS = ((0, 48), (48, 48), (96, 16), (112, 16))
COL_PARTS = ((0, 384), (384, 384), (768, 128), (896, 128))
KX_ORDER = (2, 1, 3, 0)
KZ_ORDER = (2, 1, 3, 0)


def kernel(
    q_h, kn_h, vn_h, ck_h, cv_h, clen, acc, ent_h, low_h, mid_h, wo_h, w_h, teach_h,
    high_o, grad_o,
    q_v, kn_v, vn_v, ck_v, cv_v, ent_v, wo_v, wy, flm, fh, ft, sb, sr, tb, att, joint, es, ex, ec, grad_v,
    part1, part2, gath,
    ssem, rsem, lsem,
):
    g = lax.axis_index("group")
    t = lax.axis_index("tensor")
    y, zl, c = g // 4, (g // 2) % 2, g % 2
    zh, x = t // 4, t % 4

    def dev(dy=0, dzl=0, dc=0, dz=0, dx=0):
        yy = xor4(y, dy)
        return (yy * 4 + ((zl + dzl) % 2) * 2 + (c + dc) % 2, xor4(zh, dz) * 4 + xor4(x, dx))

    sent = []
    counts = [0, 0]

    def send(src, dst, peer):
        i = counts[0]
        counts[0] += 1
        copy = pltpu.make_async_remote_copy(
            src_ref=src, dst_ref=dst, send_sem=ssem.at[i], recv_sem=rsem.at[i],
            device_id=peer, device_id_type=MESH,
        )
        copy.start()
        sent.append(copy)
        return copy

    def load(src, dst):
        i = counts[1]
        counts[1] += 1
        copy = pltpu.make_async_copy(src, dst, lsem.at[i])
        copy.start()
        return copy

    barrier = pltpu.get_barrier_semaphore()
    peers = [dict(dx=1), dict(dx=3), dict(dz=1), dict(dz=3), dict(dy=1), dict(dy=2), dict(dy=3),
             dict(dzl=1), dict(dc=1), dict(dzl=1, dc=1)]
    for p in peers:
        pl.semaphore_signal(barrier, inc=1, device_id=dev(**p), device_id_type=MESH)

    l_att = [load(q_h, q_v), load(kn_h, kn_v), load(ck_h, ck_v), load(vn_h, vn_v), load(cv_h, cv_v)]
    l_w = load(w_h, wy.at[0])
    l_f = [load(low_h, flm.at[c, y, zl, 0]), load(mid_h, flm.at[c, y, zl, 1])]
    l_wo = []
    for i, (kx, kz) in enumerate((kx, kz) for kx in KX_ORDER for kz in KZ_ORDER):
        owner = xor4(zh, kz) * 4 + xor4(x, kx)
        l_wo.append(load(wo_h.at[:, pl.ds(pl.multiple_of(owner * 512, 512), 512)], wo_v.at[i]))
    l_ent = load(ent_h, ent_v)

    total = acc[0] + acc[1] + acc[2] + acc[3]
    scale = 4.0 / jnp.full((32, 128), total, jnp.int32).astype(F32)
    place = lax.broadcasted_iota(jnp.int32, (32, 128), 0)
    sb[...] = jnp.where(place < jnp.full((32, 128), acc[x], jnp.int32), scale, 0.0)

    pl.semaphore_wait(barrier, len(peers))

    b1, b0 = zh // 2, zh % 2
    tpeer = (y * 4 + ((zl + b1) % 2) * 2 + (c + b0) % 2, t)
    tsrc = []
    for ky in range(4):
        col = (xor4(y, ky) * 4 + ((zl + b1) % 2) * 2 + (c + b0) % 2) * 256
        tsrc.append(teach_h.at[pl.ds(pl.multiple_of(x * 32, 32), 32), pl.ds(pl.multiple_of(col, 256), 256)])
    base_r, base_l = counts[0], counts[1]
    counts[0] += 5
    counts[1] += 5

    def teacher_remote(i):
        src, dst = (tsrc[i], tb.at[i]) if i < 4 else (sb, sr)
        return pltpu.make_async_remote_copy(
            src_ref=src, dst_ref=dst, send_sem=ssem.at[base_r + i], recv_sem=rsem.at[base_r + i],
            device_id=tpeer, device_id_type=MESH,
        )

    def teacher_local(i):
        src, dst = (tsrc[i], tb.at[i]) if i < 4 else (sb, sr)
        return pltpu.make_async_copy(src, dst, lsem.at[base_l + i])

    @pl.when(zh != 0)
    def _():
        for i in range(5):
            teacher_remote(i).start()

    @pl.when(zh == 0)
    def _():
        for i in range(5):
            teacher_local(i).start()

    for cp in l_f:
        cp.wait()
    lm_zl = send(flm.at[c, y, zl], flm.at[c, y, zl], dev(dzl=1))
    lm_c = send(flm.at[c, y, zl], flm.at[c, y, zl], dev(dc=1))
    l_w.wait()
    w_y1 = send(wy.at[0], wy.at[1], dev(dy=1))
    w_y3 = send(wy.at[0], wy.at[3], dev(dy=3))

    for cp in l_att:
        cp.wait()
    inv = 128 ** (-0.5)
    for s in range(4):
        rows = slice(s * 32, s * 32 + 32)
        query = jnp.concatenate([q_v[rows, h * 128 : h * 128 + 128] for h in range(4)], axis=0)
        s_cache = dot_nt(query, ck_v[s]) * inv
        s_new = dot_nt(query, kn_v[...]) * inv
        slot = lax.broadcasted_iota(jnp.int32, (128, 512), 1)
        s_cache = jnp.where(slot < clen[s], s_cache, -jnp.inf)
        col = lax.broadcasted_iota(jnp.int32, (128, 128), 1) - s * 32
        row = lax.broadcasted_iota(jnp.int32, (128, 128), 0) % 32
        s_new = jnp.where((col >= 0) & (col <= row), s_new, -jnp.inf)
        top = jnp.maximum(jnp.max(s_cache, axis=1, keepdims=True), jnp.max(s_new, axis=1, keepdims=True))
        p_cache = jnp.exp(s_cache - top)
        p_new = jnp.exp(s_new - top)
        tot = jnp.sum(p_cache, axis=1, keepdims=True) + jnp.sum(p_new, axis=1, keepdims=True)
        mixed = dot(p_cache.astype(BF16), cv_v[s]) + dot(p_new.astype(BF16), vn_v[...])
        result = (mixed / tot).astype(BF16)
        for h in range(4):
            att[rows, h * 128 : h * 128 + 128] = result[h * 32 : h * 32 + 32]

    def begin(parts):
        return [Part(parts[i * 10 : i * 10 + 10], *PARTS[i]) for i in range(4)]

    def partner(p, first, k):
        return dev(dx=k) if p.x_first == first else dev(dz=k)

    def send_1(p, j):
        return send(p.s1.at[j], p.r1.at[j], partner(p, True, p.a))

    def step_2(parts, c1b):
        out = []
        for p, cp in zip(parts, c1b):
            cp.wait_recv()
            p.s2[...] = (p.k1[1] + p.r1[1].astype(F32)).astype(BF16)
            out.append(send(p.s2, p.r2, partner(p, True, p.b)))
        return out

    def step_3(parts, c1a, c2):
        for p, cp in zip(parts, c1a):
            cp.wait_recv()
            p.k1[0] = p.k1[0] + p.r1[0].astype(F32)
        out = []
        for p, cp in zip(parts, c2):
            cp.wait_recv()
            p.s3[...] = (p.k1[0, 2:4] + p.r2[2:4].astype(F32)).astype(BF16)
            out.append(send(p.s3, p.r3, partner(p, False, p.a2)))
        for p in parts:
            p.k2[...] = p.k1[0, 0:2] + p.r2[0:2].astype(F32)
        return out

    def step_4(parts, c3):
        out = []
        for p, cp in zip(parts, c3):
            cp.wait_recv()
            p.s4[...] = (p.k2[1] + p.r3[1].astype(F32)).astype(BF16)
            out.append(send(p.s4, p.r4, partner(p, False, p.b2)))
        return out

    def final(p, cp):
        cp.wait_recv()
        return p.k2[0] + p.r3[0].astype(F32) + p.r4[...].astype(F32)

    parts = begin(part1)
    c1a, c1b = [None] * 4, [None] * 4
    a_v = att[...]
    for i, (kx, kz) in enumerate((kx, kz) for kx in KX_ORDER for kz in KZ_ORDER):
        l_wo[i].wait()
        value = dot(a_v, wo_v[i])
        for p, (start, size) in zip(parts, ROW_PARTS):
            p.store(kz, kx, slice(None), value[start : start + size])
        if i == 3:
            c1b[0], c1b[1] = send_1(parts[0], 1), send_1(parts[1], 1)
        if i == 7:
            c1a[0] = send_1(parts[0], 0)
        if i == 11:
            c1a[1] = send_1(parts[1], 0)
        if i == 12:
            c1b[2], c1b[3] = send_1(parts[2], 1), send_1(parts[3], 1)
        if i == 13:
            c1a[2] = send_1(parts[2], 0)
        if i == 14:
            c1a[3] = send_1(parts[3], 0)

    lm_zl.wait_recv()
    lm_c2 = send(flm.at[c, y, (zl + 1) % 2], flm.at[c, y, (zl + 1) % 2], dev(dc=1))
    c2 = step_2(parts, c1b)
    w_y1.wait_recv()
    w_2a = send(wy.at[1, pl.ds(0, 768)], wy.at[2, pl.ds(0, 768)], dev(dy=3))
    w_y3.wait_recv()
    w_2b = send(wy.at[3, pl.ds(768, 768)], wy.at[2, pl.ds(768, 768)], dev(dy=1))
    lm_y1 = send(flm.at[c, y], flm.at[c, y], dev(dy=1))
    lm_y3 = send(flm.at[c, y], flm.at[c, y], dev(dy=3))
    c3 = step_3(parts, c1a, c2)
    c4 = step_4(parts, c3)
    lm_c.wait_recv()
    lm_c2.wait_recv()
    w_2a.wait_recv()
    w_2b.wait_recv()
    groups = []
    for kz in range(4):
        zz = xor4(zh, kz)
        groups.append(((c + zz % 2) % 2, (zl + zz // 2) % 2))

    def join_lm(s, carry):
        rows = jnp.concatenate(
            [jnp.concatenate([flm[cc, y, zz, f, s] for f in range(2)], axis=1) for cc, zz in groups], axis=0
        )
        for ky in range(4):
            joint[s, :, ky * 256 : ky * 256 + 256] = dot(rows, wy[ky, 0:1024])
        return carry

    lax.fori_loop(0, 4, join_lm, 0)
    l_ent.wait()
    for p, cp, (start, size) in zip(parts, c4, ROW_PARTS):
        value = final(p, cp)
        value = (ent_v[start : start + size].astype(F32) + value).astype(BF16)
        for r in range(0, size, 16):
            fh[c, y, zl, (start + r) // 32, (start + r) % 32 : (start + r) % 32 + 16] = value[r : r + 16]
    h_zl = send(fh.at[c, y, zl], fh.at[c, y, zl], dev(dzl=1))
    h_c = send(fh.at[c, y, zl], fh.at[c, y, zl], dev(dc=1))
    o_high = load(fh.at[c, y, zl], high_o)
    h_zl.wait_recv()
    h_c2 = send(fh.at[c, y, (zl + 1) % 2], fh.at[c, y, (zl + 1) % 2], dev(dc=1))
    h_y1 = send(fh.at[c, y], fh.at[c, y], dev(dy=1))
    h_y3 = send(fh.at[c, y], fh.at[c, y], dev(dy=3))
    h_c.wait_recv()
    h_c2.wait_recv()

    parts = begin(part2)
    c1a, c1b = [None] * 4, [None] * 4
    for kx in KX_ORDER:
        s = xor4(x, kx)
        rows = jnp.concatenate([fh[cc, y, zz, s] for cc, zz in groups], axis=0)
        for ky in range(4):
            value = joint[s, :, ky * 256 : ky * 256 + 256] + dot(rows, wy[ky, 1024:1536])
            for half in range(2):
                at = ky * 256 + half * 128
                for p, (start, size) in zip(parts, COL_PARTS):
                    if start <= at < start + size:
                        for kz in range(4):
                            p.store(kz, kx, slice(at - start, at - start + 128),
                                    value[kz * 32 : kz * 32 + 32, half * 128 : half * 128 + 128])
        if kx == 2:
            c1b[0], c1b[1] = send_1(parts[0], 1), send_1(parts[1], 1)
        if kx == 1:
            c1a[0] = send_1(parts[0], 0)
        if kx == 3:
            c1a[1] = send_1(parts[1], 0)
    for i in (2, 3):
        c1b[i] = send_1(parts[i], 1)
    for i in (2, 3):
        c1a[i] = send_1(parts[i], 0)

    y1, y3, y2 = xor4(y, 1), xor4(y, 3), xor4(y, 2)
    lm_y1.wait_recv()
    lm_2a = send(flm.at[c, y1, 0], flm.at[c, y1, 0], dev(dy=3))
    lm_y3.wait_recv()
    lm_2b = send(flm.at[c, y3, 1], flm.at[c, y3, 1], dev(dy=1))
    lm_f = [send(flm.at[c, y1], flm.at[c, y1], dev(dc=1)), send(flm.at[c, y3], flm.at[c, y3], dev(dc=1))]
    c2 = step_2(parts, c1b)
    lm_2a.wait_recv()
    lm_2b.wait_recv()
    lm_f.append(send(flm.at[c, y2], flm.at[c, y2], dev(dc=1)))
    h_y1.wait_recv()
    h_2a = send(fh.at[c, y1, 0], fh.at[c, y1, 0], dev(dy=3))
    h_y3.wait_recv()
    h_2b = send(fh.at[c, y3, 1], fh.at[c, y3, 1], dev(dy=1))
    h_f = [send(fh.at[c, y1], fh.at[c, y1], dev(dc=1)), send(fh.at[c, y3], fh.at[c, y3], dev(dc=1))]
    c3 = step_3(parts, c1a, c2)
    for cp in lm_f:
        cp.wait_recv()

    def turn(lo, hi, feature):
        def body(j, carry):
            kx, kz = j // 4, j % 4
            zz = xor4(zh, kz)
            cc, ll = (c + zz % 2) % 2, (zl + zz // 2) % 2
            s = xor4(x, kx)
            if feature < 2:
                blocks = [flm[cc, xor4(y, ky), ll, feature, s] for ky in range(4)]
            else:
                blocks = [fh[cc, xor4(y, ky), ll, s] for ky in range(4)]
            rows = jnp.concatenate(blocks, axis=0)
            ft[feature, :, pl.ds(pl.multiple_of(j * 128, 128), 128)] = rows.T
            return carry

        lax.fori_loop(lo, hi, body, 0)

    turn(0, 6, 0)
    c4 = step_4(parts, c3)
    turn(6, 12, 0)
    h_2a.wait_recv()
    h_2b.wait_recv()
    h_f.append(send(fh.at[c, y2], fh.at[c, y2], dev(dc=1)))

    @pl.when(zh != 0)
    def _():
        for i in range(5):
            teacher_remote(i).wait()

    @pl.when(zh == 0)
    def _():
        for i in range(5):
            teacher_local(i).wait()

    row_scale = sr[...]
    for p, cp, (start, size) in zip(parts, c4, COL_PARTS):
        value = final(p, cp)
        for off in range(0, size, 128):
            at = start + off
            ky, lanes = at // 256, slice(at % 256, at % 256 + 128)
            err = (value[:, off : off + 128] - tb[ky, :, lanes].astype(F32)) * row_scale
            es[ky, :, lanes] = err.astype(BF16)
    e_y = [send(es.at[ky], ex.at[ky], dev(dy=ky)) for ky in (1, 3, 2)]
    ex[0] = es[0]
    turn(12, 16, 0)
    for cp in e_y:
        cp.wait_recv()
    for p, (start, size), gb in zip(parts, ROW_PARTS, gath):
        for r in range(0, size, 16):
            gb[0, 0, r : r + 16] = ex[(start + r) // 32, (start + r) % 32 : (start + r) % 32 + 16]
    cps = [send(gb.at[0, 0], gb.at[0, 1], partner(p, False, p.a2)) for p, gb in zip(parts, gath)]
    turn(0, 4, 1)
    for cp in cps:
        cp.wait_recv()
    cps = [send(gb.at[0, pl.ds(0, 2)], gb.at[0, pl.ds(2, 2)], partner(p, False, p.b2)) for p, gb in zip(parts, gath)]
    turn(4, 10, 1)
    for cp in cps:
        cp.wait_recv()
    cps = [send(gb.at[0], gb.at[1], partner(p, True, p.a)) for p, gb in zip(parts, gath)]
    turn(10, 16, 1)
    for cp in cps:
        cp.wait_recv()
    cps = [send(gb.at[pl.ds(0, 2)], gb.at[pl.ds(2, 2)], partner(p, True, p.b)) for p, gb in zip(parts, gath)]
    for cp in h_f:
        cp.wait_recv()
    turn(0, 16, 2)
    for cp in cps:
        cp.wait_recv()

    def slot(p, gb, kz, kx):
        first, second = (kx, kz) if p.x_first else (kz, kx)
        return gb[(0, p.a, p.b, 2).index(first), (0, p.a2, p.b2, 2).index(second)]

    for kx in range(4):
        for kz in range(4):
            j = kx * 4 + kz
            ec[j * 128 : j * 128 + 128] = jnp.concatenate(
                [slot(p, gb, kz, kx) for p, gb in zip(parts, gath)], axis=0
            )
    outs = []
    for f in range(3):
        grad_v[f] = dot(ft[f], ec[...])
        outs.append(load(grad_v.at[f], grad_o.at[f]))
    for cp in outs:
        cp.wait()
    o_high.wait()
    for cp in sent:
        cp.wait_send()


def shards(
    queries, keys_new, values_new, cache_keys, cache_values, cache_len, accepted,
    entering, low_feature, mid_feature, out_proj, join_weight, teacher,
):
    anywhere = pl.BlockSpec(memory_space=pl.ANY)
    scalars = pl.BlockSpec(memory_space=pltpu.SMEM)
    scratch = [
        pltpu.VMEM((128, 512), BF16),
        pltpu.VMEM((128, 128), BF16),
        pltpu.VMEM((128, 128), BF16),
        pltpu.VMEM((4, 512, 128), BF16),
        pltpu.VMEM((4, 512, 128), BF16),
        pltpu.VMEM((128, 512), BF16),
        pltpu.VMEM((16, 512, 512), BF16),
        pltpu.VMEM((4, 1536, 256), BF16),
        pltpu.VMEM((2, 4, 2, 2, 4, 32, 512), BF16),
        pltpu.VMEM((2, 4, 2, 4, 32, 512), BF16),
        pltpu.VMEM((3, 512, 2048), BF16),
        pltpu.VMEM((32, 128), F32),
        pltpu.VMEM((32, 128), F32),
        pltpu.VMEM((4, 32, 256), BF16),
        pltpu.VMEM((128, 512), BF16),
        pltpu.VMEM((4, 128, 1024), F32),
        pltpu.VMEM((4, 32, 256), BF16),
        pltpu.VMEM((4, 32, 256), BF16),
        pltpu.VMEM((2048, 256), BF16),
        pltpu.VMEM((3, 512, 256), F32),
        [s for _, size in ROW_PARTS for s in part_shapes(size, 512)],
        [s for _, size in COL_PARTS for s in part_shapes(32, size)],
        [pltpu.VMEM((4, 4, size, 256), BF16) for _, size in ROW_PARTS],
        pltpu.SemaphoreType.DMA((COPIES,)),
        pltpu.SemaphoreType.DMA((COPIES,)),
        pltpu.SemaphoreType.DMA((LOADS,)),
    ]
    high, grad = pl.pallas_call(
        kernel,
        out_shape=(
            jax.ShapeDtypeStruct((4, 32, 512), BF16),
            jax.ShapeDtypeStruct((3, 512, 256), F32),
        ),
        in_specs=[anywhere] * 5 + [scalars] * 2 + [anywhere] * 6,
        out_specs=(anywhere, anywhere),
        scratch_shapes=scratch,
        compiler_params=pltpu.CompilerParams(
            collective_id=0, has_side_effects=True, vmem_limit_bytes=60 * 2**20
        ),
        name="verify_join",
    )(
        queries, keys_new, values_new, cache_keys.reshape(4, 512, 128), cache_values.reshape(4, 512, 128),
        cache_len, accepted, entering, low_feature.reshape(4, 32, 512), mid_feature.reshape(4, 32, 512),
        out_proj, join_weight.reshape(1536, 256), teacher,
    )
    return high.reshape(128, 512), grad


def solution(mesh):
    return jax.shard_map(
        shards,
        mesh=mesh,
        in_specs=(
            P("group", "tensor"),
            P("group", "tensor"),
            P("group", "tensor"),
            P("group", "tensor", None, None),
            P("group", "tensor", None, None),
            P("group"),
            P("group"),
            P("group", "tensor"),
            P("group", "tensor"),
            P("group", "tensor"),
            P("tensor", None),
            P(None, "tensor", "group"),
            P("group", None),
        ),
        out_specs=(P("group", "tensor"), P(None, "tensor", "group")),
        check_vma=False,
    )
```

```python
import jax
import jax.numpy as jnp
from jax import lax
from jax.experimental import pallas as pl
from jax.experimental.pallas import tpu as pltpu
from jax.sharding import PartitionSpec as P

MESH = pl.DeviceIdType.MESH
F32 = jnp.float32
BF16 = jnp.bfloat16
COPIES = 160
LOADS = 96
OTHER = {1: 3, 3: 1}


def xor4(v, k):
    return ((v // 2 + k // 2) % 2) * 2 + (v % 2 + k % 2) % 2


def dot(a, b):
    return jnp.dot(a, b, preferred_element_type=F32)


def dot_nt(a, b):
    return lax.dot_general(a, b, (((1,), (1,)), ((), ())), preferred_element_type=F32)


class Part:
    def __init__(self, bufs, x_first, a, a2):
        self.s1, self.r1, self.k1, self.s2, self.r2, self.k2, self.s3, self.r3, self.s4, self.r4 = bufs
        self.x_first, self.a, self.b, self.a2, self.b2 = x_first, a, OTHER[a], a2, OTHER[a2]
        self.order1 = (0, self.b, a, 2)
        self.order2 = (0, self.b2, a2, 2)

    def place(self, kz, kx):
        first, second = (kx, kz) if self.x_first else (kz, kx)
        return self.order1.index(first), self.order2.index(second)

    def store(self, kz, kx, columns, value):
        first, second = self.place(kz, kx)
        if first >= 2:
            self.s1[first - 2, second, :, columns] = value.astype(BF16)
        else:
            self.k1[first, second, :, columns] = value


def part_shapes(rows, width):
    return [
        pltpu.VMEM((2, 4, rows, width), BF16),
        pltpu.VMEM((2, 4, rows, width), BF16),
        pltpu.VMEM((2, 4, rows, width), F32),
        pltpu.VMEM((4, rows, width), BF16),
        pltpu.VMEM((4, rows, width), BF16),
        pltpu.VMEM((2, rows, width), F32),
        pltpu.VMEM((2, rows, width), BF16),
        pltpu.VMEM((2, rows, width), BF16),
        pltpu.VMEM((rows, width), BF16),
        pltpu.VMEM((rows, width), BF16),
    ]


PARTS = ((True, 1, 1), (True, 3, 3), (False, 1, 1), (False, 3, 3))
ROW_PARTS = ((0, 48), (48, 48), (96, 16), (112, 16))
KX_ORDER = (2, 1, 3, 0)
KZ_ORDER = (2, 1, 3, 0)


def kernel(
    q_h, kn_h, vn_h, ck_h, cv_h, clen, acc, ent_h, low_h, mid_h, wo_h, w_h, teach_h,
    high_o, grad_o,
    q_v, kn_v, vn_v, ck_v, cv_v, ent_v, wo_v, wy, flm, fh, ft, sb, sr, tb, att, joint, xs, xr, zk, zs, zr, es, gath,
    grad_v, part1,
    ssem, rsem, lsem,
):
    g = lax.axis_index("group")
    t = lax.axis_index("tensor")
    y, zl, c = g // 4, (g // 2) % 2, g % 2
    zh, x = t // 4, t % 4

    def dev(dy=0, dzl=0, dc=0, dz=0, dx=0):
        yy = xor4(y, dy)
        return (yy * 4 + ((zl + dzl) % 2) * 2 + (c + dc) % 2, xor4(zh, dz) * 4 + xor4(x, dx))

    sent = []
    counts = [0, 0]

    def send(src, dst, peer):
        i = counts[0]
        counts[0] += 1
        copy = pltpu.make_async_remote_copy(
            src_ref=src, dst_ref=dst, send_sem=ssem.at[i], recv_sem=rsem.at[i],
            device_id=peer, device_id_type=MESH,
        )
        copy.start()
        sent.append(copy)
        return copy

    def load(src, dst):
        i = counts[1]
        counts[1] += 1
        copy = pltpu.make_async_copy(src, dst, lsem.at[i])
        copy.start()
        return copy

    barrier = pltpu.get_barrier_semaphore()
    peers = [dict(dx=1), dict(dx=2), dict(dx=3), dict(dz=1), dict(dz=2), dict(dz=3), dict(dy=1), dict(dy=2), dict(dy=3),
             dict(dzl=1), dict(dc=1), dict(dzl=1, dc=1)]
    for p in peers:
        pl.semaphore_signal(barrier, inc=1, device_id=dev(**p), device_id_type=MESH)

    l_att = [load(q_h, q_v), load(kn_h, kn_v), load(ck_h, ck_v), load(vn_h, vn_v), load(cv_h, cv_v)]
    l_w = load(w_h, wy.at[0])
    l_f = [load(low_h, flm.at[c, y, zl, 0]), load(mid_h, flm.at[c, y, zl, 1])]
    l_wo = []
    for i, (kx, kz) in enumerate((kx, kz) for kx in KX_ORDER for kz in KZ_ORDER):
        owner = xor4(zh, kz) * 4 + xor4(x, kx)
        l_wo.append(load(wo_h.at[:, pl.ds(pl.multiple_of(owner * 512, 512), 512)], wo_v.at[i]))
    l_ent = load(ent_h, ent_v)

    total = acc[0] + acc[1] + acc[2] + acc[3]
    scale = 4.0 / jnp.full((32, 128), total, jnp.int32).astype(F32)
    place = lax.broadcasted_iota(jnp.int32, (32, 128), 0)
    sb[...] = jnp.where(place < jnp.full((32, 128), acc[x], jnp.int32), scale, 0.0)

    inv = 128 ** (-0.5)

    def attend(s):
        rows = slice(s * 32, s * 32 + 32)
        query = jnp.concatenate([q_v[rows, h * 128 : h * 128 + 128] for h in range(4)], axis=0)
        s_cache = dot_nt(query, ck_v[s]) * inv
        s_new = dot_nt(query, kn_v[...]) * inv
        slot = lax.broadcasted_iota(jnp.int32, (128, 512), 1)
        s_cache = jnp.where(slot < clen[s], s_cache, -jnp.inf)
        col = lax.broadcasted_iota(jnp.int32, (128, 128), 1) - s * 32
        row = lax.broadcasted_iota(jnp.int32, (128, 128), 0) % 32
        s_new = jnp.where((col >= 0) & (col <= row), s_new, -jnp.inf)
        top = jnp.maximum(jnp.max(s_cache, axis=1, keepdims=True), jnp.max(s_new, axis=1, keepdims=True))
        p_cache = jnp.exp(s_cache - top)
        p_new = jnp.exp(s_new - top)
        tot = jnp.sum(p_cache, axis=1, keepdims=True) + jnp.sum(p_new, axis=1, keepdims=True)
        mixed = dot(p_cache.astype(BF16), cv_v[s]) + dot(p_new.astype(BF16), vn_v[...])
        result = (mixed / tot).astype(BF16)
        for h in range(4):
            att[rows, h * 128 : h * 128 + 128] = result[h * 32 : h * 32 + 32]

    for cp in l_att:
        cp.wait()
    attend(0)
    pl.semaphore_wait(barrier, len(peers))
    w_y1 = send(w_h, wy.at[1], dev(dy=1))
    w_y3 = send(w_h, wy.at[3], dev(dy=3))

    b1, b0 = zh // 2, zh % 2
    tpeer = (y * 4 + ((zl + b1) % 2) * 2 + (c + b0) % 2, t)
    tsrc = []
    for ky in range(4):
        col = (xor4(y, ky) * 4 + ((zl + b1) % 2) * 2 + (c + b0) % 2) * 256
        tsrc.append(teach_h.at[pl.ds(pl.multiple_of(x * 32, 32), 32), pl.ds(pl.multiple_of(col, 256), 256)])
    base_r, base_l = counts[0], counts[1]
    counts[0] += 5
    counts[1] += 5

    def teacher_remote(i):
        src, dst = (tsrc[i], tb.at[i]) if i < 4 else (sb, sr)
        return pltpu.make_async_remote_copy(
            src_ref=src, dst_ref=dst, send_sem=ssem.at[base_r + i], recv_sem=rsem.at[base_r + i],
            device_id=tpeer, device_id_type=MESH,
        )

    def teacher_local(i):
        src, dst = (tsrc[i], tb.at[i]) if i < 4 else (sb, sr)
        return pltpu.make_async_copy(src, dst, lsem.at[base_l + i])

    @pl.when(zh != 0)
    def _():
        for i in range(5):
            teacher_remote(i).start()

    @pl.when(zh == 0)
    def _():
        for i in range(5):
            teacher_local(i).start()

    for cp in l_f:
        cp.wait()
    lm_zl = send(flm.at[c, y, zl], flm.at[c, y, zl], dev(dzl=1))
    lm_c = send(flm.at[c, y, zl], flm.at[c, y, zl], dev(dc=1))

    for s in range(1, 4):
        attend(s)

    def begin(parts):
        return [Part(parts[i * 10 : i * 10 + 10], *PARTS[i]) for i in range(4)]

    def partner(p, first, k):
        return dev(dx=k) if p.x_first == first else dev(dz=k)

    def send_1(p, j):
        return send(p.s1.at[j], p.r1.at[j], partner(p, True, p.a))

    def step_2(parts, c1b):
        out = []
        for p, cp in zip(parts, c1b):
            cp.wait_recv()
            p.s2[...] = (p.k1[1] + p.r1[1].astype(F32)).astype(BF16)
            out.append(send(p.s2, p.r2, partner(p, True, p.b)))
        return out

    def step_3(parts, c1a, c2):
        for p, cp in zip(parts, c1a):
            cp.wait_recv()
            p.k1[0] = p.k1[0] + p.r1[0].astype(F32)
        out = []
        for p, cp in zip(parts, c2):
            cp.wait_recv()
            p.s3[...] = (p.k1[0, 2:4] + p.r2[2:4].astype(F32)).astype(BF16)
            out.append(send(p.s3, p.r3, partner(p, False, p.a2)))
        for p in parts:
            p.k2[...] = p.k1[0, 0:2] + p.r2[0:2].astype(F32)
        return out

    def step_4(parts, c3):
        out = []
        for p, cp in zip(parts, c3):
            cp.wait_recv()
            p.s4[...] = (p.k2[1] + p.r3[1].astype(F32)).astype(BF16)
            out.append(send(p.s4, p.r4, partner(p, False, p.b2)))
        return out

    def final(p, cp):
        cp.wait_recv()
        return p.k2[0] + p.r3[0].astype(F32) + p.r4[...].astype(F32)

    parts = begin(part1)
    c1a, c1b = [None] * 4, [None] * 4
    a_v = att[...]
    for i, (kx, kz) in enumerate((kx, kz) for kx in KX_ORDER for kz in KZ_ORDER):
        l_wo[i].wait()
        value = dot(a_v, wo_v[i])
        for p, (start, size) in zip(parts, ROW_PARTS):
            p.store(kz, kx, slice(None), value[start : start + size])
        if i == 3:
            c1b[0], c1b[1] = send_1(parts[0], 1), send_1(parts[1], 1)
        if i == 7:
            c1a[0] = send_1(parts[0], 0)
        if i == 11:
            c1a[1] = send_1(parts[1], 0)
        if i == 12:
            c1b[2], c1b[3] = send_1(parts[2], 1), send_1(parts[3], 1)
        if i == 13:
            c1a[2] = send_1(parts[2], 0)
        if i == 14:
            c1a[3] = send_1(parts[3], 0)

    lm_zl.wait_recv()
    lm_c2 = send(flm.at[c, y, (zl + 1) % 2], flm.at[c, y, (zl + 1) % 2], dev(dc=1))
    c2 = step_2(parts, c1b)
    w_y1.wait_recv()
    w_2a = send(wy.at[1, pl.ds(0, 768)], wy.at[2, pl.ds(0, 768)], dev(dy=3))
    w_y3.wait_recv()
    w_2b = send(wy.at[3, pl.ds(768, 768)], wy.at[2, pl.ds(768, 768)], dev(dy=1))
    c3 = step_3(parts, c1a, c2)
    c4 = step_4(parts, c3)
    lm_c.wait_recv()
    lm_c2.wait_recv()
    l_w.wait()
    w_2a.wait_recv()
    w_2b.wait_recv()
    lm_y1 = send(flm.at[c, y], flm.at[c, y], dev(dy=1))
    lm_y3 = send(flm.at[c, y], flm.at[c, y], dev(dy=3))
    groups = [((c + j % 2) % 2, (zl + j // 2) % 2) for j in range(4)]
    for j, (cc, ll) in enumerate(groups):
        rows = jnp.concatenate([flm[cc, y, ll, f].reshape(128, 512) for f in range(2)], axis=1)
        for ky in range(4):
            joint[j, :, :, ky * 256 : ky * 256 + 256] = dot(rows, wy[ky, 0:1024]).reshape(4, 32, 256)
    l_ent.wait()
    for p, cp, (start, size) in zip(parts, c4, ROW_PARTS):
        value = final(p, cp)
        value = (ent_v[start : start + size].astype(F32) + value).astype(BF16)
        for r in range(0, size, 16):
            fh[c, y, zl, (start + r) // 32, (start + r) % 32 : (start + r) % 32 + 16] = value[r : r + 16]
    h_zl = send(fh.at[c, y, zl], fh.at[c, y, zl], dev(dzl=1))
    h_c = send(fh.at[c, y, zl], fh.at[c, y, zl], dev(dc=1))
    o_high = load(fh.at[c, y, zl], high_o)

    to_x = [None] * 4

    def join(j):
        cc, ll = groups[j]
        rows = fh[cc, y, ll].reshape(128, 512)
        for ky in range(4):
            cols = slice(ky * 256, ky * 256 + 256)
            value = joint[j, :, :, cols] + dot(rows, wy[ky, 1024:1536]).reshape(4, 32, 256)
            joint[j, :, :, cols] = value
            xs[j, :, :, cols] = value.astype(BF16)
        to_x[j] = [send(xs.at[j, xor4(x, k)], xr.at[j, k], dev(dx=k)) for k in (2, 1, 3)]

    base_z = counts[0]
    counts[0] += 8

    def to_z(j):
        k = xor4(zh, j)
        return pltpu.make_async_remote_copy(
            src_ref=zs.at[j], dst_ref=zr.at[k], send_sem=ssem.at[base_z + j], recv_sem=rsem.at[base_z + 4 + k],
            device_id=(g, j * 4 + x), device_id_type=MESH,
        )

    def sum_x(j):
        value = joint[j, x]
        for cp, k in zip(to_x[j], (2, 1, 3)):
            cp.wait_recv()
        for k in (1, 2, 3):
            value = value + xr[j, k].astype(F32)
        zk[j] = value
        zs[j] = value.astype(BF16)

        @pl.when(zh != j)
        def _():
            to_z(j).start()

    join(0)
    h_c.wait_recv()
    join(1)
    h_zl.wait_recv()
    h_c2 = send(fh.at[c, y, (zl + 1) % 2], fh.at[c, y, (zl + 1) % 2], dev(dc=1))
    join(2)
    sum_x(0)
    h_c2.wait_recv()
    join(3)
    h_y1 = send(fh.at[c, y], fh.at[c, y], dev(dy=1))
    h_y3 = send(fh.at[c, y], fh.at[c, y], dev(dy=3))
    sum_x(1)
    sum_x(2)
    sum_x(3)

    y1, y3, y2 = xor4(y, 1), xor4(y, 3), xor4(y, 2)
    lm_y1.wait_recv()
    lm_2a = send(flm.at[c, y1, 0], flm.at[c, y1, 0], dev(dy=3))
    lm_y3.wait_recv()
    lm_2b = send(flm.at[c, y3, 1], flm.at[c, y3, 1], dev(dy=1))
    lm_f = [send(flm.at[c, y1], flm.at[c, y1], dev(dc=1)), send(flm.at[c, y3], flm.at[c, y3], dev(dc=1))]

    def turn(lo, hi, feature):
        def body(j, carry):
            kz, kx = j // 4, j % 4
            zz = xor4(zh, kz)
            cc, ll = (c + zz % 2) % 2, (zl + zz // 2) % 2
            s = xor4(x, kx)
            if feature < 2:
                blocks = [flm[cc, xor4(y, ky), ll, feature, s] for ky in range(4)]
            else:
                blocks = [fh[cc, xor4(y, ky), ll, s] for ky in range(4)]
            rows = jnp.concatenate(blocks, axis=0)
            ft[feature, :, pl.ds(pl.multiple_of(j * 128, 128), 128)] = rows.T
            return carry

        lax.fori_loop(lo, hi, body, 0)

    @pl.when(zh != 0)
    def _():
        for i in range(5):
            teacher_remote(i).wait()

    @pl.when(zh == 0)
    def _():
        for i in range(5):
            teacher_local(i).wait()

    value = zk[zh]
    for k in (1, 3, 2):
        pltpu.make_async_remote_copy(
            src_ref=zs.at[0], dst_ref=zr.at[k], send_sem=ssem.at[base_z], recv_sem=rsem.at[base_z + 4 + k],
            device_id=dev(dz=k), device_id_type=MESH,
        ).wait_recv()
        value = value + zr[k].astype(F32)
    row_scale = jnp.concatenate([sr[...], sr[...]], axis=1)
    for ky in (1, 3, 2, 0):
        err = (value[:, ky * 256 : ky * 256 + 256] - tb[ky].astype(F32)) * row_scale
        if ky:
            es[ky] = err.astype(BF16)
        else:
            gath[0, 0, 0] = err.astype(BF16)
    e_y = [send(es.at[ky], gath.at[0, 0, ky], dev(dy=ky)) for ky in (1, 3, 2)]
    e_z0 = {k: send(gath.at[0, 0, 0], gath.at[k, 0, 0], dev(dz=k)) for k in (2, 1, 3)}
    for cp in e_y:
        cp.wait_recv()
    rest = pl.ds(1, 3)
    e_z1 = {k: send(gath.at[0, 0, rest], gath.at[k, 0, rest], dev(dz=k)) for k in (2, 1, 3)}
    e_x = {0: [send(gath.at[0, 0], gath.at[0, k], dev(dx=k)) for k in (2, 1, 3)]}
    h_y1.wait_recv()
    h_2a = send(fh.at[c, y1, 0], fh.at[c, y1, 0], dev(dy=3))
    h_y3.wait_recv()
    h_2b = send(fh.at[c, y3, 1], fh.at[c, y3, 1], dev(dy=1))
    h_f = [send(fh.at[c, y1], fh.at[c, y1], dev(dc=1)), send(fh.at[c, y3], fh.at[c, y3], dev(dc=1))]
    lm_2a.wait_recv()
    lm_2b.wait_recv()
    lm_f.append(send(flm.at[c, y2], flm.at[c, y2], dev(dc=1)))
    for k in (1, 3):
        e_z0[k].wait_recv()
        e_z1[k].wait_recv()
        e_x[k] = [send(gath.at[k, 0], gath.at[k, q], dev(dx=q)) for q in (2, 1, 3)]
    e_z0[2].wait_recv()
    e_z1[2].wait_recv()
    e_x[2] = [send(gath.at[2, 0], gath.at[2, q], dev(dx=q)) for q in (2, 1, 3)]
    h_2a.wait_recv()
    h_2b.wait_recv()
    h_f.append(send(fh.at[c, y2], fh.at[c, y2], dev(dc=1)))
    for cp in lm_f:
        cp.wait_recv()
    turn(0, 16, 0)
    turn(0, 16, 1)
    for cp in h_f:
        cp.wait_recv()
    turn(0, 16, 2)

    outs = []
    for k in (0, 1, 3, 2):
        for cp in e_x[k]:
            cp.wait_recv()
        block = gath[k].reshape(512, 256)
        for f in range(3):
            value = dot(ft[f, :, k * 512 : k * 512 + 512], block)
            if k:
                value = grad_v[f] + value
            grad_v[f] = value
            if k == 2:
                outs.append(load(grad_v.at[f], grad_o.at[f]))
    for cp in outs:
        cp.wait()
    o_high.wait()
    for cp in sent:
        cp.wait_send()
    for j in range(4):

        @pl.when(zh != j)
        def _():
            to_z(j).wait_send()


def deliver(high_i, grad_i, high_o, grad_o, high_v, grad_v, sem):
    ins = [pltpu.make_async_copy(high_i, high_v, sem.at[0, 0])]
    outs = [pltpu.make_async_copy(high_v, high_o, sem.at[1, 0])]
    for f in range(3):
        ins.append(pltpu.make_async_copy(grad_i.at[f], grad_v.at[f], sem.at[0, f + 1]))
        outs.append(pltpu.make_async_copy(grad_v.at[f], grad_o.at[f], sem.at[1, f + 1]))
    for copy in ins:
        copy.start()
    for before, after in zip(ins, outs):
        before.wait()
        after.start()
    for copy in outs:
        copy.wait()


def shards(
    queries, keys_new, values_new, cache_keys, cache_values, cache_len, accepted,
    entering, low_feature, mid_feature, out_proj, join_weight, teacher,
):
    anywhere = pl.BlockSpec(memory_space=pl.ANY)
    far = pl.BlockSpec(memory_space=pltpu.HBM)
    scalars = pl.BlockSpec(memory_space=pltpu.SMEM)
    scratch = [
        pltpu.VMEM((128, 512), BF16),
        pltpu.VMEM((128, 128), BF16),
        pltpu.VMEM((128, 128), BF16),
        pltpu.VMEM((4, 512, 128), BF16),
        pltpu.VMEM((4, 512, 128), BF16),
        pltpu.VMEM((128, 512), BF16),
        pltpu.VMEM((16, 512, 512), BF16),
        pltpu.VMEM((4, 1536, 256), BF16),
        pltpu.VMEM((2, 4, 2, 2, 4, 32, 512), BF16),
        pltpu.VMEM((2, 4, 2, 4, 32, 512), BF16),
        pltpu.VMEM((3, 512, 2048), BF16),
        pltpu.VMEM((32, 128), F32),
        pltpu.VMEM((32, 128), F32),
        pltpu.VMEM((4, 32, 256), BF16),
        pltpu.VMEM((128, 512), BF16),
        pltpu.VMEM((4, 4, 32, 1024), F32),
        pltpu.VMEM((4, 4, 32, 1024), BF16),
        pltpu.VMEM((4, 4, 32, 1024), BF16),
        pltpu.VMEM((4, 32, 1024), F32),
        pltpu.VMEM((4, 32, 1024), BF16),
        pltpu.VMEM((4, 32, 1024), BF16),
        pltpu.VMEM((4, 32, 256), BF16),
        pltpu.VMEM((4, 4, 4, 32, 256), BF16),
        pltpu.VMEM((3, 512, 256), F32),
        [s for _, size in ROW_PARTS for s in part_shapes(size, 512)],
        pltpu.SemaphoreType.DMA((COPIES,)),
        pltpu.SemaphoreType.DMA((COPIES,)),
        pltpu.SemaphoreType.DMA((LOADS,)),
    ]
    high, grad = pl.pallas_call(
        kernel,
        out_shape=(
            jax.ShapeDtypeStruct((4, 32, 512), BF16),
            jax.ShapeDtypeStruct((3, 512, 256), F32),
        ),
        in_specs=[far] * 5 + [scalars] * 2 + [far] * 6,
        out_specs=(anywhere, anywhere),
        scratch_shapes=scratch,
        compiler_params=pltpu.CompilerParams(
            collective_id=0, has_side_effects=True, vmem_limit_bytes=60 * 2**20
        ),
        name="verify_join",
    )(
        queries, keys_new, values_new, cache_keys.reshape(4, 512, 128), cache_values.reshape(4, 512, 128),
        cache_len, accepted, entering, low_feature.reshape(4, 32, 512), mid_feature.reshape(4, 32, 512),
        out_proj, join_weight.reshape(1536, 256), teacher,
    )
    high, grad = pl.pallas_call(
        deliver,
        out_shape=(
            jax.ShapeDtypeStruct((4, 32, 512), BF16),
            jax.ShapeDtypeStruct((3, 512, 256), F32),
        ),
        in_specs=[anywhere] * 2,
        out_specs=(anywhere, anywhere),
        scratch_shapes=[
            pltpu.VMEM((4, 32, 512), BF16),
            pltpu.VMEM((3, 512, 256), F32),
            pltpu.SemaphoreType.DMA((2, 4)),
        ],
        compiler_params=pltpu.CompilerParams(vmem_limit_bytes=60 * 2**20),
        name="deliver",
    )(high, grad)
    return high.reshape(128, 512), grad


def solution(mesh):
    return jax.shard_map(
        shards,
        mesh=mesh,
        in_specs=(
            P("group", "tensor"),
            P("group", "tensor"),
            P("group", "tensor"),
            P("group", "tensor", None, None),
            P("group", "tensor", None, None),
            P("group"),
            P("group"),
            P("group", "tensor"),
            P("group", "tensor"),
            P("group", "tensor"),
            P("tensor", None),
            P(None, "tensor", "group"),
            P("group", None),
        ),
        out_specs=(P("group", "tensor"), P(None, "tensor", "group")),
        check_vma=False,
    )
```

```python
import jax
import jax.numpy as jnp
from jax import lax
from jax.experimental import pallas as pl
from jax.experimental.pallas import tpu as pltpu
from jax.sharding import PartitionSpec as P

MESH = pl.DeviceIdType.MESH
F32 = jnp.float32
BF16 = jnp.bfloat16
COPIES = 192
LOADS = 96
OTHER = {1: 3, 3: 1}


def xor4(v, k):
    return ((v // 2 + k // 2) % 2) * 2 + (v % 2 + k % 2) % 2


def dot(a, b):
    return jnp.dot(a, b, preferred_element_type=F32)


def dot_nt(a, b):
    return lax.dot_general(a, b, (((1,), (1,)), ((), ())), preferred_element_type=F32)


class Part:
    def __init__(self, bufs, x_first, a, a2):
        self.s1, self.r1, self.k1, self.s2, self.r2, self.k2, self.s3, self.r3, self.s4, self.r4 = bufs
        self.x_first, self.a, self.b, self.a2, self.b2 = x_first, a, OTHER[a], a2, OTHER[a2]
        self.order1 = (0, self.b, a, 2)
        self.order2 = (0, self.b2, a2, 2)

    def place(self, kz, kx):
        first, second = (kx, kz) if self.x_first else (kz, kx)
        return self.order1.index(first), self.order2.index(second)

    def store(self, kz, kx, columns, value):
        first, second = self.place(kz, kx)
        if first >= 2:
            self.s1[first - 2, second, :, columns] = value.astype(BF16)
        else:
            self.k1[first, second, :, columns] = value


def part_shapes(rows, width):
    return [
        pltpu.VMEM((2, 4, rows, width), BF16),
        pltpu.VMEM((2, 4, rows, width), BF16),
        pltpu.VMEM((2, 4, rows, width), F32),
        pltpu.VMEM((4, rows, width), BF16),
        pltpu.VMEM((4, rows, width), BF16),
        pltpu.VMEM((2, rows, width), F32),
        pltpu.VMEM((2, rows, width), BF16),
        pltpu.VMEM((2, rows, width), BF16),
        pltpu.VMEM((rows, width), BF16),
        pltpu.VMEM((rows, width), BF16),
    ]


PARTS = ((True, 1, 1), (True, 3, 3), (False, 1, 1), (False, 3, 3))
ROW_PARTS = ((0, 48), (48, 48), (96, 16), (112, 16))
KX_ORDER = (2, 1, 3, 0)
KZ_ORDER = (2, 1, 3, 0)


def kernel(
    q_h, kn_h, vn_h, ck_h, cv_h, clen, acc, ent_h, low_h, mid_h, wo_h, w_h, teach_h,
    high_o, grad_o,
    q_v, kn_v, vn_v, ck_v, cv_v, ent_v, wo_v, wy, flm, fh, ft, sr, tb, att, joint, xs, xr, zk, zs, zr, es, gath,
    grad_v, part1,
    ssem, rsem, lsem,
):
    g = lax.axis_index("group")
    t = lax.axis_index("tensor")
    y, zl, c = g // 4, (g // 2) % 2, g % 2
    zh, x = t // 4, t % 4

    def dev(dy=0, dzl=0, dc=0, dz=0, dx=0):
        yy = xor4(y, dy)
        return (yy * 4 + ((zl + dzl) % 2) * 2 + (c + dc) % 2, xor4(zh, dz) * 4 + xor4(x, dx))

    sent = []
    counts = [0, 0]

    def send(src, dst, peer):
        i = counts[0]
        counts[0] += 1
        copy = pltpu.make_async_remote_copy(
            src_ref=src, dst_ref=dst, send_sem=ssem.at[i], recv_sem=rsem.at[i],
            device_id=peer, device_id_type=MESH,
        )
        copy.start()
        sent.append(copy)
        return copy

    def load(src, dst):
        i = counts[1]
        counts[1] += 1
        copy = pltpu.make_async_copy(src, dst, lsem.at[i])
        copy.start()
        return copy

    barrier = pltpu.get_barrier_semaphore()
    peers = [dict(dx=1), dict(dx=2), dict(dx=3), dict(dz=1), dict(dz=2), dict(dz=3), dict(dy=1), dict(dy=3),
             dict(dzl=1), dict(dc=1), dict(dzl=1, dc=1)]
    for p in peers:
        pl.semaphore_signal(barrier, inc=1, device_id=dev(**p), device_id_type=MESH)

    def error_source(ky):
        return ((xor4(y, ky) * 4 + zl * 2 + c), y * 4 + x)

    for ky in (1, 2, 3):
        pl.semaphore_signal(barrier, inc=1, device_id=error_source(ky), device_id_type=MESH)

    @pl.when(zh != y)
    def _():
        pl.semaphore_signal(barrier, inc=1, device_id=error_source(0), device_id_type=MESH)

    l_att = [load(q_h, q_v), load(kn_h, kn_v), load(ck_h, ck_v), load(vn_h, vn_v), load(cv_h, cv_v)]
    l_w = load(w_h, wy.at[0])
    l_f = [load(low_h, flm.at[c, y, zl, 0]), load(mid_h, flm.at[c, y, zl, 1])]
    l_wo = []
    for i, (kx, kz) in enumerate((kx, kz) for kx in KX_ORDER for kz in KZ_ORDER):
        owner = xor4(zh, kz) * 4 + xor4(x, kx)
        l_wo.append(load(wo_h.at[:, pl.ds(pl.multiple_of(owner * 512, 512), 512)], wo_v.at[i]))
    l_ent = load(ent_h, ent_v)

    total = acc[0] + acc[1] + acc[2] + acc[3]
    scale = 4.0 / jnp.full((32, 128), total, jnp.int32).astype(F32)
    place = lax.broadcasted_iota(jnp.int32, (32, 128), 0)
    sr[0] = jnp.where(place < jnp.full((32, 128), acc[x], jnp.int32), scale, 0.0)

    inv = 128 ** (-0.5)

    def attend(s):
        rows = slice(s * 32, s * 32 + 32)
        query = jnp.concatenate([q_v[rows, h * 128 : h * 128 + 128] for h in range(4)], axis=0)
        s_cache = dot_nt(query, ck_v[s]) * inv
        s_new = dot_nt(query, kn_v[...]) * inv
        slot = lax.broadcasted_iota(jnp.int32, (128, 512), 1)
        s_cache = jnp.where(slot < clen[s], s_cache, -jnp.inf)
        col = lax.broadcasted_iota(jnp.int32, (128, 128), 1) - s * 32
        row = lax.broadcasted_iota(jnp.int32, (128, 128), 0) % 32
        s_new = jnp.where((col >= 0) & (col <= row), s_new, -jnp.inf)
        top = jnp.maximum(jnp.max(s_cache, axis=1, keepdims=True), jnp.max(s_new, axis=1, keepdims=True))
        p_cache = jnp.exp(s_cache - top)
        p_new = jnp.exp(s_new - top)
        tot = jnp.sum(p_cache, axis=1, keepdims=True) + jnp.sum(p_new, axis=1, keepdims=True)
        mixed = dot(p_cache.astype(BF16), cv_v[s]) + dot(p_new.astype(BF16), vn_v[...])
        result = (mixed / tot).astype(BF16)
        for h in range(4):
            att[rows, h * 128 : h * 128 + 128] = result[h * 32 : h * 32 + 32]

    for cp in l_att:
        cp.wait()
    attend(0)
    pl.semaphore_wait(barrier, len(peers) + 3 + (xor4(y, zh) + 3) // 4)
    w_y1 = send(w_h, wy.at[1], dev(dy=1))
    w_y3 = send(w_h, wy.at[3], dev(dy=3))

    near = (dict(), dict(dc=1), dict(dzl=1), dict(dzl=1, dc=1))

    def teacher_block(j):
        col = (zh * 4 + ((zl + j // 2) % 2) * 2 + (c + j % 2) % 2) * 256
        return teach_h.at[pl.ds(pl.multiple_of(x * 32, 32), 32), pl.ds(pl.multiple_of(col, 256), 256)]

    l_t = load(teacher_block(0), tb.at[0])
    got_t = [send(teacher_block(j), tb.at[j], dev(**near[j])) for j in (1, 2, 3)]
    got_t += [send(sr.at[0], sr.at[j], dev(**near[j])) for j in (1, 2, 3)]
    for cp in l_f:
        cp.wait()
    lm_zl = send(flm.at[c, y, zl], flm.at[c, y, zl], dev(dzl=1))
    lm_c = send(flm.at[c, y, zl], flm.at[c, y, zl], dev(dc=1))

    for s in range(1, 4):
        attend(s)

    def begin(parts):
        return [Part(parts[i * 10 : i * 10 + 10], *PARTS[i]) for i in range(4)]

    def partner(p, first, k):
        return dev(dx=k) if p.x_first == first else dev(dz=k)

    def send_1(p, j):
        return send(p.s1.at[j], p.r1.at[j], partner(p, True, p.a))

    def step_2(parts, c1b):
        out = []
        for p, cp in zip(parts, c1b):
            cp.wait_recv()
            p.s2[...] = (p.k1[1] + p.r1[1].astype(F32)).astype(BF16)
            out.append(send(p.s2, p.r2, partner(p, True, p.b)))
        return out

    def step_3(parts, c1a, c2):
        for p, cp in zip(parts, c1a):
            cp.wait_recv()
            p.k1[0] = p.k1[0] + p.r1[0].astype(F32)
        out = []
        for p, cp in zip(parts, c2):
            cp.wait_recv()
            p.s3[...] = (p.k1[0, 2:4] + p.r2[2:4].astype(F32)).astype(BF16)
            out.append(send(p.s3, p.r3, partner(p, False, p.a2)))
        for p in parts:
            p.k2[...] = p.k1[0, 0:2] + p.r2[0:2].astype(F32)
        return out

    def step_4(parts, c3):
        out = []
        for p, cp in zip(parts, c3):
            cp.wait_recv()
            p.s4[...] = (p.k2[1] + p.r3[1].astype(F32)).astype(BF16)
            out.append(send(p.s4, p.r4, partner(p, False, p.b2)))
        return out

    def final(p, cp):
        cp.wait_recv()
        return p.k2[0] + p.r3[0].astype(F32) + p.r4[...].astype(F32)

    parts = begin(part1)
    c1a, c1b = [None] * 4, [None] * 4
    a_v = att[...]
    for i, (kx, kz) in enumerate((kx, kz) for kx in KX_ORDER for kz in KZ_ORDER):
        l_wo[i].wait()
        value = dot(a_v, wo_v[i])
        for p, (start, size) in zip(parts, ROW_PARTS):
            p.store(kz, kx, slice(None), value[start : start + size])
        if i == 3:
            c1b[0], c1b[1] = send_1(parts[0], 1), send_1(parts[1], 1)
        if i == 7:
            c1a[0] = send_1(parts[0], 0)
        if i == 11:
            c1a[1] = send_1(parts[1], 0)
        if i == 12:
            c1b[2], c1b[3] = send_1(parts[2], 1), send_1(parts[3], 1)
        if i == 13:
            c1a[2] = send_1(parts[2], 0)
        if i == 14:
            c1a[3] = send_1(parts[3], 0)

    lm_zl.wait_recv()
    lm_c2 = send(flm.at[c, y, (zl + 1) % 2], flm.at[c, y, (zl + 1) % 2], dev(dc=1))
    c2 = step_2(parts, c1b)
    w_y1.wait_recv()
    w_2a = send(wy.at[1, pl.ds(0, 768)], wy.at[2, pl.ds(0, 768)], dev(dy=3))
    w_y3.wait_recv()
    w_2b = send(wy.at[3, pl.ds(768, 768)], wy.at[2, pl.ds(768, 768)], dev(dy=1))
    c3 = step_3(parts, c1a, c2)
    c4 = step_4(parts, c3)
    lm_c.wait_recv()
    lm_c2.wait_recv()
    l_w.wait()
    w_2a.wait_recv()
    w_2b.wait_recv()
    lm_y1 = send(flm.at[c, y], flm.at[c, y], dev(dy=1))
    lm_y3 = send(flm.at[c, y], flm.at[c, y], dev(dy=3))
    groups = [((c + j % 2) % 2, (zl + j // 2) % 2) for j in range(4)]
    for j, (cc, ll) in enumerate(groups):
        rows = jnp.concatenate([flm[cc, y, ll, f].reshape(128, 512) for f in range(2)], axis=1)
        for ky in range(4):
            joint[j, :, ky] = dot(rows, wy[ky, 0:1024]).reshape(4, 32, 256)
    l_ent.wait()
    for p, cp, (start, size) in zip(parts, c4, ROW_PARTS):
        value = final(p, cp)
        value = (ent_v[start : start + size].astype(F32) + value).astype(BF16)
        for r in range(0, size, 16):
            fh[c, y, zl, (start + r) // 32, (start + r) % 32 : (start + r) % 32 + 16] = value[r : r + 16]
    h_zl = send(fh.at[c, y, zl], fh.at[c, y, zl], dev(dzl=1))
    h_c = send(fh.at[c, y, zl], fh.at[c, y, zl], dev(dc=1))
    o_high = load(fh.at[c, y, zl], high_o)

    own_ky = xor4(y, zh)
    to_x, to_x2 = [None] * 4, [None] * 4

    def join(j):
        cc, ll = groups[j]
        rows = fh[cc, y, ll].reshape(128, 512)
        for ky in range(4):
            value = joint[j, :, ky] + dot(rows, wy[ky, 1024:1536]).reshape(4, 32, 256)
            joint[j, :, ky] = value
            xs[j, :, ky] = value.astype(BF16)
        to_x[j] = [send(xs.at[j, xor4(x, k)], xr.at[j, k], dev(dx=k)) for k in (2, 1, 3)]

    to_z = [None] * 4

    def sum_x(j):
        for cp in to_x[j]:
            cp.wait_recv()
        value = joint[j, x]
        for k in (1, 2, 3):
            value = value + xr[j, k].astype(F32)
        zk[j] = value
        zs[j] = value.astype(BF16)
        to_z[j] = [send(zs.at[j, xor4(own_ky, k)], zr.at[j, k], dev(dz=k)) for k in (2, 1, 3)]

    base_e = counts[0]
    counts[0] += 32

    def error_copy(j, kz, ky):
        return pltpu.make_async_remote_copy(
            src_ref=es.at[j], dst_ref=gath.at[j, 0, ky],
            send_sem=ssem.at[base_e + j * 4 + kz], recv_sem=rsem.at[base_e + 16 + j * 4 + ky],
            device_id=(zh * 4 + zl * 2 + c, xor4(zh, kz) * 4 + x), device_id_type=MESH,
        )

    def error(j):
        for cp in to_z[j]:
            cp.wait_recv()
        value = zk[j, own_ky]
        for k in (1, 2, 3):
            value = value + zr[j, k].astype(F32)
        row_scale = jnp.concatenate([sr[j], sr[j]], axis=1)
        err = ((value - tb[j].astype(F32)) * row_scale).astype(BF16)
        es[j] = err
        for kz in (2, 1, 3):
            error_copy(j, kz, own_ky).start()

        @pl.when(zh != y)
        def _():
            error_copy(j, 0, own_ky).start()

        @pl.when(zh == y)
        def _():
            gath[j, 0, 0] = es[j]

    def spread(j):
        for ky in (1, 3, 2):
            error_copy(j, 0, ky).wait_recv()

        @pl.when(zh != y)
        def _():
            error_copy(j, 0, 0).wait_recv()

        to_x2[j] = [send(gath.at[j, 0], gath.at[j, k], dev(dx=k)) for k in (2, 1, 3)]

    def turn(lo, hi, feature):
        def body(i, carry):
            j, s = i // 4, xor4(x, i % 4)
            cc, ll = (c + j % 2) % 2, (zl + j // 2) % 2
            if feature < 2:
                blocks = [flm[cc, xor4(y, ky), ll, feature, s] for ky in range(4)]
            else:
                blocks = [fh[cc, xor4(y, ky), ll, s] for ky in range(4)]
            rows = jnp.concatenate(blocks, axis=0)
            ft[feature, :, pl.ds(pl.multiple_of(i * 128, 128), 128)] = rows.T
            return carry

        lax.fori_loop(lo, hi, body, 0)

    y1, y3, y2 = xor4(y, 1), xor4(y, 3), xor4(y, 2)
    join(0)
    h_c.wait_recv()
    join(1)
    h_zl.wait_recv()
    h_c2 = send(fh.at[c, y, (zl + 1) % 2], fh.at[c, y, (zl + 1) % 2], dev(dc=1))
    join(2)
    h_y1 = send(fh.at[c, y], fh.at[c, y], dev(dy=1))
    h_y3 = send(fh.at[c, y], fh.at[c, y], dev(dy=3))
    sum_x(0)
    sum_x(1)
    h_c2.wait_recv()
    join(3)
    l_t.wait()
    for cp in got_t:
        cp.wait_recv()
    error(0)
    sum_x(2)
    error(1)
    lm_y1.wait_recv()
    lm_2a = send(flm.at[c, y1, 0], flm.at[c, y1, 0], dev(dy=3))
    lm_y3.wait_recv()
    lm_2b = send(flm.at[c, y3, 1], flm.at[c, y3, 1], dev(dy=1))
    sum_x(3)
    lm_f = [send(flm.at[c, y1], flm.at[c, y1], dev(dc=1)), send(flm.at[c, y3], flm.at[c, y3], dev(dc=1))]
    spread(0)
    error(2)
    spread(1)
    error(3)
    h_y1.wait_recv()
    h_2a = send(fh.at[c, y1, 0], fh.at[c, y1, 0], dev(dy=3))
    h_y3.wait_recv()
    h_2b = send(fh.at[c, y3, 1], fh.at[c, y3, 1], dev(dy=1))
    h_f = [send(fh.at[c, y1], fh.at[c, y1], dev(dc=1)), send(fh.at[c, y3], fh.at[c, y3], dev(dc=1))]
    spread(2)
    lm_2a.wait_recv()
    lm_2b.wait_recv()
    lm_f.append(send(flm.at[c, y2], flm.at[c, y2], dev(dc=1)))
    spread(3)
    for f in (0, 1):
        turn(0, 4, f)
        turn(8, 12, f)
    h_2a.wait_recv()
    h_2b.wait_recv()
    h_f.append(send(fh.at[c, y2], fh.at[c, y2], dev(dc=1)))
    for cp in lm_f:
        cp.wait_recv()
    for f in (0, 1):
        turn(4, 8, f)
        turn(12, 16, f)
    outs = []

    def grow(j):
        for cp in to_x2[j]:
            cp.wait_recv()
        block = gath[j].reshape(512, 256)
        for f in range(3):
            value = dot(ft[f, :, j * 512 : j * 512 + 512], block)
            if j:
                value = grad_v[f] + value
            grad_v[f] = value
            if j == 3:
                outs.append(load(grad_v.at[f], grad_o.at[f]))

    turn(0, 4, 2)
    grow(0)
    turn(8, 12, 2)
    grow(2)
    for cp in h_f:
        cp.wait_recv()
    turn(4, 8, 2)
    grow(1)
    turn(12, 16, 2)
    grow(3)
    for cp in outs:
        cp.wait()
    o_high.wait()
    for cp in sent:
        cp.wait_send()
    for j in range(4):
        for kz in (1, 2, 3):
            error_copy(j, kz, own_ky).wait_send()

    @pl.when(zh != y)
    def _():
        for j in range(4):
            error_copy(j, 0, own_ky).wait_send()


def deliver(high_i, grad_i, high_o, grad_o, high_v, grad_v, sem):
    ins = [pltpu.make_async_copy(high_i, high_v, sem.at[0, 0])]
    outs = [pltpu.make_async_copy(high_v, high_o, sem.at[1, 0])]
    for f in range(3):
        ins.append(pltpu.make_async_copy(grad_i.at[f], grad_v.at[f], sem.at[0, f + 1]))
        outs.append(pltpu.make_async_copy(grad_v.at[f], grad_o.at[f], sem.at[1, f + 1]))
    for copy in ins:
        copy.start()
    for before, after in zip(ins, outs):
        before.wait()
        after.start()
    for copy in outs:
        copy.wait()


def shards(
    queries, keys_new, values_new, cache_keys, cache_values, cache_len, accepted,
    entering, low_feature, mid_feature, out_proj, join_weight, teacher,
):
    anywhere = pl.BlockSpec(memory_space=pl.ANY)
    far = pl.BlockSpec(memory_space=pltpu.HBM)
    scalars = pl.BlockSpec(memory_space=pltpu.SMEM)
    scratch = [
        pltpu.VMEM((128, 512), BF16),
        pltpu.VMEM((128, 128), BF16),
        pltpu.VMEM((128, 128), BF16),
        pltpu.VMEM((4, 512, 128), BF16),
        pltpu.VMEM((4, 512, 128), BF16),
        pltpu.VMEM((128, 512), BF16),
        pltpu.VMEM((16, 512, 512), BF16),
        pltpu.VMEM((4, 1536, 256), BF16),
        pltpu.VMEM((2, 4, 2, 2, 4, 32, 512), BF16),
        pltpu.VMEM((2, 4, 2, 4, 32, 512), BF16),
        pltpu.VMEM((3, 512, 2048), BF16),
        pltpu.VMEM((4, 32, 128), F32),
        pltpu.VMEM((4, 32, 256), BF16),
        pltpu.VMEM((128, 512), BF16),
        pltpu.VMEM((4, 4, 4, 32, 256), F32),
        pltpu.VMEM((4, 4, 4, 32, 256), BF16),
        pltpu.VMEM((4, 4, 4, 32, 256), BF16),
        pltpu.VMEM((4, 4, 32, 256), F32),
        pltpu.VMEM((4, 4, 32, 256), BF16),
        pltpu.VMEM((4, 4, 32, 256), BF16),
        pltpu.VMEM((4, 32, 256), BF16),
        pltpu.VMEM((4, 4, 4, 32, 256), BF16),
        pltpu.VMEM((3, 512, 256), F32),
        [s for _, size in ROW_PARTS for s in part_shapes(size, 512)],
        pltpu.SemaphoreType.DMA((COPIES,)),
        pltpu.SemaphoreType.DMA((COPIES,)),
        pltpu.SemaphoreType.DMA((LOADS,)),
    ]
    high, grad = pl.pallas_call(
        kernel,
        out_shape=(
            jax.ShapeDtypeStruct((4, 32, 512), BF16),
            jax.ShapeDtypeStruct((3, 512, 256), F32),
        ),
        in_specs=[far] * 5 + [scalars] * 2 + [far] * 6,
        out_specs=(anywhere, anywhere),
        scratch_shapes=scratch,
        compiler_params=pltpu.CompilerParams(
            collective_id=0, has_side_effects=True, vmem_limit_bytes=60 * 2**20
        ),
        name="verify_join",
    )(
        queries, keys_new, values_new, cache_keys.reshape(4, 512, 128), cache_values.reshape(4, 512, 128),
        cache_len, accepted, entering, low_feature.reshape(4, 32, 512), mid_feature.reshape(4, 32, 512),
        out_proj, join_weight.reshape(1536, 256), teacher,
    )
    high, grad = pl.pallas_call(
        deliver,
        out_shape=(
            jax.ShapeDtypeStruct((4, 32, 512), BF16),
            jax.ShapeDtypeStruct((3, 512, 256), F32),
        ),
        in_specs=[anywhere] * 2,
        out_specs=(anywhere, anywhere),
        scratch_shapes=[
            pltpu.VMEM((4, 32, 512), BF16),
            pltpu.VMEM((3, 512, 256), F32),
            pltpu.SemaphoreType.DMA((2, 4)),
        ],
        compiler_params=pltpu.CompilerParams(vmem_limit_bytes=60 * 2**20),
        name="deliver",
    )(high, grad)
    return high.reshape(128, 512), grad


def solution(mesh):
    return jax.shard_map(
        shards,
        mesh=mesh,
        in_specs=(
            P("group", "tensor"),
            P("group", "tensor"),
            P("group", "tensor"),
            P("group", "tensor", None, None),
            P("group", "tensor", None, None),
            P("group"),
            P("group"),
            P("group", "tensor"),
            P("group", "tensor"),
            P("group", "tensor"),
            P("tensor", None),
            P(None, "tensor", "group"),
            P("group", None),
        ),
        out_specs=(P("group", "tensor"), P(None, "tensor", "group")),
        check_vma=False,
    )
```

```python
import jax
import jax.numpy as jnp
from jax import lax
from jax.experimental import pallas as pl
from jax.experimental.pallas import tpu as pltpu
from jax.sharding import PartitionSpec as P

MESH = pl.DeviceIdType.MESH
F32 = jnp.float32
BF16 = jnp.bfloat16
COPIES = 192
LOADS = 96
OTHER = {1: 3, 3: 1}


def xor4(v, k):
    return ((v // 2 + k // 2) % 2) * 2 + (v % 2 + k % 2) % 2


def dot(a, b):
    return jnp.dot(a, b, preferred_element_type=F32)


def dot_nt(a, b):
    return lax.dot_general(a, b, (((1,), (1,)), ((), ())), preferred_element_type=F32)


class Part:
    def __init__(self, bufs, x_first, a, a2):
        self.s1, self.r1, self.k1, self.s2, self.r2, self.k2, self.s3, self.r3, self.s4, self.r4 = bufs
        self.x_first, self.a, self.b, self.a2, self.b2 = x_first, a, OTHER[a], a2, OTHER[a2]
        self.order1 = (0, self.b, a, 2)
        self.order2 = (0, self.b2, a2, 2)

    def place(self, kz, kx):
        first, second = (kx, kz) if self.x_first else (kz, kx)
        return self.order1.index(first), self.order2.index(second)

    def store(self, kz, kx, columns, value):
        first, second = self.place(kz, kx)
        if first >= 2:
            self.s1[first - 2, second, :, columns] = value.astype(BF16)
        else:
            self.k1[first, second, :, columns] = value


def part_shapes(rows, width):
    return [
        pltpu.VMEM((2, 4, rows, width), BF16),
        pltpu.VMEM((2, 4, rows, width), BF16),
        pltpu.VMEM((2, 4, rows, width), F32),
        pltpu.VMEM((4, rows, width), BF16),
        pltpu.VMEM((4, rows, width), BF16),
        pltpu.VMEM((2, rows, width), F32),
        pltpu.VMEM((2, rows, width), BF16),
        pltpu.VMEM((2, rows, width), BF16),
        pltpu.VMEM((rows, width), BF16),
        pltpu.VMEM((rows, width), BF16),
    ]


PARTS = ((True, 1, 1), (True, 3, 3), (False, 1, 1), (False, 3, 3))
ROW_PARTS = ((0, 48), (48, 48), (96, 16), (112, 16))
KX_ORDER = (2, 1, 3, 0)
KZ_ORDER = (2, 1, 3, 0)


def kernel(
    q_h, kn_h, vn_h, ck_h, cv_h, clen, acc, ent_h, low_h, mid_h, wo_h, w_h, teach_h,
    high_o, grad_o,
    q_v, kn_v, vn_v, ck_v, cv_v, ent_v, wo_v, wy, flm, fh, ft, sr, tb, att, joint, xs, xr, zk, zs, zr, es, gath,
    grad_v, part1,
    ssem, rsem, lsem,
):
    g = lax.axis_index("group")
    t = lax.axis_index("tensor")
    y, zl, c = g // 4, (g // 2) % 2, g % 2
    zh, x = t // 4, t % 4

    def dev(dy=0, dzl=0, dc=0, dz=0, dx=0):
        yy = xor4(y, dy)
        return (yy * 4 + ((zl + dzl) % 2) * 2 + (c + dc) % 2, xor4(zh, dz) * 4 + xor4(x, dx))

    sent = []
    counts = [0, 0]

    def send(src, dst, peer):
        i = counts[0]
        counts[0] += 1
        copy = pltpu.make_async_remote_copy(
            src_ref=src, dst_ref=dst, send_sem=ssem.at[i], recv_sem=rsem.at[i],
            device_id=peer, device_id_type=MESH,
        )
        copy.start()
        sent.append(copy)
        return copy

    def load(src, dst):
        i = counts[1]
        counts[1] += 1
        copy = pltpu.make_async_copy(src, dst, lsem.at[i])
        copy.start()
        return copy

    barrier = pltpu.get_barrier_semaphore()
    peers = [dict(dx=1), dict(dx=2), dict(dx=3), dict(dz=1), dict(dz=2), dict(dz=3), dict(dy=1), dict(dy=3),
             dict(dzl=1), dict(dc=1), dict(dzl=1, dc=1)]
    for p in peers:
        pl.semaphore_signal(barrier, inc=1, device_id=dev(**p), device_id_type=MESH)

    def error_source(ky):
        return ((xor4(y, ky) * 4 + zl * 2 + c), y * 4 + x)

    for ky in (1, 2, 3):
        pl.semaphore_signal(barrier, inc=1, device_id=error_source(ky), device_id_type=MESH)

    @pl.when(zh != y)
    def _():
        pl.semaphore_signal(barrier, inc=1, device_id=error_source(0), device_id_type=MESH)

    l_att = [load(q_h, q_v), load(kn_h, kn_v), load(ck_h, ck_v), load(vn_h, vn_v), load(cv_h, cv_v)]
    l_w = load(w_h, wy.at[0])
    l_f = [load(low_h, flm.at[c, y, zl, 0]), load(mid_h, flm.at[c, y, zl, 1])]
    l_wo = []
    for i, (kx, kz) in enumerate((kx, kz) for kx in KX_ORDER for kz in KZ_ORDER):
        owner = xor4(zh, kz) * 4 + xor4(x, kx)
        l_wo.append(load(wo_h.at[:, pl.ds(pl.multiple_of(owner * 512, 512), 512)], wo_v.at[i]))
    l_ent = load(ent_h, ent_v)

    total = acc[0] + acc[1] + acc[2] + acc[3]
    scale = 4.0 / jnp.full((32, 128), total, jnp.int32).astype(F32)
    place = lax.broadcasted_iota(jnp.int32, (32, 128), 0)
    sr[0] = jnp.where(place < jnp.full((32, 128), acc[x], jnp.int32), scale, 0.0)

    pl.semaphore_wait(barrier, len(peers) + 3 + (xor4(y, zh) + 3) // 4)
    w_y1 = send(w_h, wy.at[1], dev(dy=1))
    w_y3 = send(w_h, wy.at[3], dev(dy=3))
    inv = 128 ** (-0.5)

    def attend(s):
        rows = slice(s * 32, s * 32 + 32)
        query = jnp.concatenate([q_v[rows, h * 128 : h * 128 + 128] for h in range(4)], axis=0)
        s_cache = dot_nt(query, ck_v[s]) * inv
        s_new = dot_nt(query, kn_v[...]) * inv
        slot = lax.broadcasted_iota(jnp.int32, (128, 512), 1)
        s_cache = jnp.where(slot < clen[s], s_cache, -jnp.inf)
        col = lax.broadcasted_iota(jnp.int32, (128, 128), 1) - s * 32
        row = lax.broadcasted_iota(jnp.int32, (128, 128), 0) % 32
        s_new = jnp.where((col >= 0) & (col <= row), s_new, -jnp.inf)
        top = jnp.maximum(jnp.max(s_cache, axis=1, keepdims=True), jnp.max(s_new, axis=1, keepdims=True))
        p_cache = jnp.exp(s_cache - top)
        p_new = jnp.exp(s_new - top)
        tot = jnp.sum(p_cache, axis=1, keepdims=True) + jnp.sum(p_new, axis=1, keepdims=True)
        mixed = dot(p_cache.astype(BF16), cv_v[s]) + dot(p_new.astype(BF16), vn_v[...])
        result = (mixed / tot).astype(BF16)
        for h in range(4):
            att[rows, h * 128 : h * 128 + 128] = result[h * 32 : h * 32 + 32]

    for cp in l_att:
        cp.wait()
    attend(0)

    near = (dict(), dict(dc=1), dict(dzl=1), dict(dzl=1, dc=1))

    def teacher_block(j):
        col = (zh * 4 + ((zl + j // 2) % 2) * 2 + (c + j % 2) % 2) * 256
        return teach_h.at[pl.ds(pl.multiple_of(x * 32, 32), 32), pl.ds(pl.multiple_of(col, 256), 256)]

    l_t = load(teacher_block(0), tb.at[0])
    got_t = [send(teacher_block(j), tb.at[j], dev(**near[j])) for j in (1, 2, 3)]
    got_t += [send(sr.at[0], sr.at[j], dev(**near[j])) for j in (1, 2, 3)]
    for cp in l_f:
        cp.wait()
    lm_zl = send(flm.at[c, y, zl], flm.at[c, y, zl], dev(dzl=1))
    lm_c = send(flm.at[c, y, zl], flm.at[c, y, zl], dev(dc=1))

    for s in range(1, 4):
        attend(s)

    def begin(parts):
        return [Part(parts[i * 10 : i * 10 + 10], *PARTS[i]) for i in range(4)]

    def partner(p, first, k):
        return dev(dx=k) if p.x_first == first else dev(dz=k)

    def send_1(p, j):
        return send(p.s1.at[j], p.r1.at[j], partner(p, True, p.a))

    def step_2(parts, c1b):
        out = []
        for p, cp in zip(parts, c1b):
            cp.wait_recv()
            p.s2[...] = (p.k1[1] + p.r1[1].astype(F32)).astype(BF16)
            out.append(send(p.s2, p.r2, partner(p, True, p.b)))
        return out

    def step_3(parts, c1a, c2):
        for p, cp in zip(parts, c1a):
            cp.wait_recv()
            p.k1[0] = p.k1[0] + p.r1[0].astype(F32)
        out = []
        for p, cp in zip(parts, c2):
            cp.wait_recv()
            p.s3[...] = (p.k1[0, 2:4] + p.r2[2:4].astype(F32)).astype(BF16)
            out.append(send(p.s3, p.r3, partner(p, False, p.a2)))
        for p in parts:
            p.k2[...] = p.k1[0, 0:2] + p.r2[0:2].astype(F32)
        return out

    def step_4(parts, c3):
        out = []
        for p, cp in zip(parts, c3):
            cp.wait_recv()
            p.s4[...] = (p.k2[1] + p.r3[1].astype(F32)).astype(BF16)
            out.append(send(p.s4, p.r4, partner(p, False, p.b2)))
        return out

    def final(p, cp):
        cp.wait_recv()
        return p.k2[0] + p.r3[0].astype(F32) + p.r4[...].astype(F32)

    parts = begin(part1)
    c1a, c1b = [None] * 4, [None] * 4
    a_v = att[...]
    for i, (kx, kz) in enumerate((kx, kz) for kx in KX_ORDER for kz in KZ_ORDER):
        l_wo[i].wait()
        value = dot(a_v, wo_v[i])
        for p, (start, size) in zip(parts, ROW_PARTS):
            p.store(kz, kx, slice(None), value[start : start + size])
        if i == 3:
            c1b[0], c1b[1] = send_1(parts[0], 1), send_1(parts[1], 1)
        if i == 7:
            c1a[0] = send_1(parts[0], 0)
        if i == 11:
            c1a[1] = send_1(parts[1], 0)
        if i == 12:
            c1b[2], c1b[3] = send_1(parts[2], 1), send_1(parts[3], 1)
        if i == 13:
            c1a[2] = send_1(parts[2], 0)
        if i == 14:
            c1a[3] = send_1(parts[3], 0)

    lm_zl.wait_recv()
    lm_c2 = send(flm.at[c, y, (zl + 1) % 2], flm.at[c, y, (zl + 1) % 2], dev(dc=1))
    c2 = step_2(parts, c1b)
    w_y1.wait_recv()
    w_2a = send(wy.at[1, pl.ds(0, 768)], wy.at[2, pl.ds(0, 768)], dev(dy=3))
    w_y3.wait_recv()
    w_2b = send(wy.at[3, pl.ds(768, 768)], wy.at[2, pl.ds(768, 768)], dev(dy=1))
    c3 = step_3(parts, c1a, c2)
    c4 = step_4(parts, c3)
    lm_c.wait_recv()
    lm_c2.wait_recv()
    l_w.wait()
    w_2a.wait_recv()
    w_2b.wait_recv()
    lm_y1 = send(flm.at[c, y], flm.at[c, y], dev(dy=1))
    lm_y3 = send(flm.at[c, y], flm.at[c, y], dev(dy=3))
    groups = [((c + j % 2) % 2, (zl + j // 2) % 2) for j in range(4)]
    for j, (cc, ll) in enumerate(groups):
        rows = jnp.concatenate([flm[cc, y, ll, f].reshape(128, 512) for f in range(2)], axis=1)
        for ky in range(4):
            joint[j, :, ky] = dot(rows, wy[ky, 0:1024]).reshape(4, 32, 256)
    l_ent.wait()
    for p, cp, (start, size) in zip(parts, c4, ROW_PARTS):
        value = final(p, cp)
        value = (ent_v[start : start + size].astype(F32) + value).astype(BF16)
        for r in range(0, size, 16):
            fh[c, y, zl, (start + r) // 32, (start + r) % 32 : (start + r) % 32 + 16] = value[r : r + 16]
    h_zl = send(fh.at[c, y, zl], fh.at[c, y, zl], dev(dzl=1))
    h_c = send(fh.at[c, y, zl], fh.at[c, y, zl], dev(dc=1))
    o_high = load(fh.at[c, y, zl], high_o)

    own_ky = xor4(y, zh)
    to_x, to_x2 = [None] * 4, [None] * 4

    def join(j):
        cc, ll = groups[j]
        rows = fh[cc, y, ll].reshape(128, 512)
        for ky in range(4):
            value = joint[j, :, ky] + dot(rows, wy[ky, 1024:1536]).reshape(4, 32, 256)
            joint[j, :, ky] = value
            xs[j, :, ky] = value.astype(BF16)
        to_x[j] = [send(xs.at[j, xor4(x, k)], xr.at[j, k], dev(dx=k)) for k in (2, 1, 3)]

    to_z = [None] * 4

    def sum_x(j):
        for cp in to_x[j]:
            cp.wait_recv()
        value = joint[j, x]
        for k in (1, 2, 3):
            value = value + xr[j, k].astype(F32)
        zk[j] = value
        zs[j] = value.astype(BF16)
        to_z[j] = [send(zs.at[j, xor4(own_ky, k)], zr.at[j, k], dev(dz=k)) for k in (2, 1, 3)]

    base_e = counts[0]
    counts[0] += 32

    def error_copy(j, kz, ky):
        return pltpu.make_async_remote_copy(
            src_ref=es.at[j], dst_ref=gath.at[j, 0, ky],
            send_sem=ssem.at[base_e + j * 4 + kz], recv_sem=rsem.at[base_e + 16 + j * 4 + ky],
            device_id=(zh * 4 + zl * 2 + c, xor4(zh, kz) * 4 + x), device_id_type=MESH,
        )

    def error(j):
        for cp in to_z[j]:
            cp.wait_recv()
        value = zk[j, own_ky]
        for k in (1, 2, 3):
            value = value + zr[j, k].astype(F32)
        row_scale = jnp.concatenate([sr[j], sr[j]], axis=1)
        err = ((value - tb[j].astype(F32)) * row_scale).astype(BF16)
        es[j] = err
        for kz in (2, 1, 3):
            error_copy(j, kz, own_ky).start()

        @pl.when(zh != y)
        def _():
            error_copy(j, 0, own_ky).start()

        @pl.when(zh == y)
        def _():
            gath[j, 0, 0] = es[j]

    def spread(j):
        for ky in (1, 3, 2):
            error_copy(j, 0, ky).wait_recv()

        @pl.when(zh != y)
        def _():
            error_copy(j, 0, 0).wait_recv()

        to_x2[j] = [send(gath.at[j, 0], gath.at[j, k], dev(dx=k)) for k in (2, 1, 3)]

    def turn(lo, hi, feature):
        def body(i, carry):
            j, s = i // 4, xor4(x, i % 4)
            cc, ll = (c + j % 2) % 2, (zl + j // 2) % 2
            if feature < 2:
                blocks = [flm[cc, xor4(y, ky), ll, feature, s] for ky in range(4)]
            else:
                blocks = [fh[cc, xor4(y, ky), ll, s] for ky in range(4)]
            rows = jnp.concatenate(blocks, axis=0)
            ft[feature, :, pl.ds(pl.multiple_of(i * 128, 128), 128)] = rows.T
            return carry

        lax.fori_loop(lo, hi, body, 0)

    y1, y3, y2 = xor4(y, 1), xor4(y, 3), xor4(y, 2)
    join(0)
    h_c.wait_recv()
    join(1)
    h_zl.wait_recv()
    h_c2 = send(fh.at[c, y, (zl + 1) % 2], fh.at[c, y, (zl + 1) % 2], dev(dc=1))
    h_y1 = send(fh.at[c, y], fh.at[c, y], dev(dy=1))
    h_y3 = send(fh.at[c, y], fh.at[c, y], dev(dy=3))
    join(2)
    sum_x(0)
    sum_x(1)
    h_c2.wait_recv()
    join(3)
    l_t.wait()
    for cp in got_t:
        cp.wait_recv()
    error(0)
    sum_x(2)
    error(1)
    lm_y1.wait_recv()
    lm_2a = send(flm.at[c, y1, 0], flm.at[c, y1, 0], dev(dy=3))
    lm_y3.wait_recv()
    lm_2b = send(flm.at[c, y3, 1], flm.at[c, y3, 1], dev(dy=1))
    sum_x(3)
    lm_f = [send(flm.at[c, y1], flm.at[c, y1], dev(dc=1)), send(flm.at[c, y3], flm.at[c, y3], dev(dc=1))]
    spread(0)
    error(2)
    spread(1)
    error(3)
    h_y1.wait_recv()
    h_2a = send(fh.at[c, y1, 0], fh.at[c, y1, 0], dev(dy=3))
    h_y3.wait_recv()
    h_2b = send(fh.at[c, y3, 1], fh.at[c, y3, 1], dev(dy=1))
    h_f = [send(fh.at[c, y1], fh.at[c, y1], dev(dc=1)), send(fh.at[c, y3], fh.at[c, y3], dev(dc=1))]
    spread(2)
    lm_2a.wait_recv()
    lm_2b.wait_recv()
    lm_f.append(send(flm.at[c, y2], flm.at[c, y2], dev(dc=1)))
    spread(3)
    for f in (0, 1):
        turn(0, 4, f)
        turn(8, 12, f)
    h_2a.wait_recv()
    h_2b.wait_recv()
    h_f.append(send(fh.at[c, y2], fh.at[c, y2], dev(dc=1)))
    for cp in lm_f:
        cp.wait_recv()
    for f in (0, 1):
        turn(4, 8, f)
        turn(12, 16, f)
    outs = []

    def grow(j):
        for cp in to_x2[j]:
            cp.wait_recv()
        block = gath[j].reshape(512, 256)
        for f in range(3):
            value = dot(ft[f, :, j * 512 : j * 512 + 512], block)
            if j:
                value = grad_v[f] + value
            grad_v[f] = value
            if j == 3:
                outs.append(load(grad_v.at[f], grad_o.at[f]))

    turn(0, 4, 2)
    grow(0)
    turn(8, 12, 2)
    grow(2)
    for cp in h_f:
        cp.wait_recv()
    turn(4, 8, 2)
    grow(1)
    turn(12, 16, 2)
    grow(3)
    for cp in outs:
        cp.wait()
    o_high.wait()
    for cp in sent:
        cp.wait_send()
    for j in range(4):
        for kz in (1, 2, 3):
            error_copy(j, kz, own_ky).wait_send()

    @pl.when(zh != y)
    def _():
        for j in range(4):
            error_copy(j, 0, own_ky).wait_send()


def deliver(high_i, grad_i, high_o, grad_o, high_v, grad_v, sem):
    ins = [pltpu.make_async_copy(high_i, high_v, sem.at[0, 0])]
    outs = [pltpu.make_async_copy(high_v, high_o, sem.at[1, 0])]
    for f in range(3):
        ins.append(pltpu.make_async_copy(grad_i.at[f], grad_v.at[f], sem.at[0, f + 1]))
        outs.append(pltpu.make_async_copy(grad_v.at[f], grad_o.at[f], sem.at[1, f + 1]))
    for copy in ins:
        copy.start()
    for before, after in zip(ins, outs):
        before.wait()
        after.start()
    for copy in outs:
        copy.wait()


def shards(
    queries, keys_new, values_new, cache_keys, cache_values, cache_len, accepted,
    entering, low_feature, mid_feature, out_proj, join_weight, teacher,
):
    anywhere = pl.BlockSpec(memory_space=pl.ANY)
    far = pl.BlockSpec(memory_space=pltpu.HBM)
    scalars = pl.BlockSpec(memory_space=pltpu.SMEM)
    scratch = [
        pltpu.VMEM((128, 512), BF16),
        pltpu.VMEM((128, 128), BF16),
        pltpu.VMEM((128, 128), BF16),
        pltpu.VMEM((4, 512, 128), BF16),
        pltpu.VMEM((4, 512, 128), BF16),
        pltpu.VMEM((128, 512), BF16),
        pltpu.VMEM((16, 512, 512), BF16),
        pltpu.VMEM((4, 1536, 256), BF16),
        pltpu.VMEM((2, 4, 2, 2, 4, 32, 512), BF16),
        pltpu.VMEM((2, 4, 2, 4, 32, 512), BF16),
        pltpu.VMEM((3, 512, 2048), BF16),
        pltpu.VMEM((4, 32, 128), F32),
        pltpu.VMEM((4, 32, 256), BF16),
        pltpu.VMEM((128, 512), BF16),
        pltpu.VMEM((4, 4, 4, 32, 256), F32),
        pltpu.VMEM((4, 4, 4, 32, 256), BF16),
        pltpu.VMEM((4, 4, 4, 32, 256), BF16),
        pltpu.VMEM((4, 4, 32, 256), F32),
        pltpu.VMEM((4, 4, 32, 256), BF16),
        pltpu.VMEM((4, 4, 32, 256), BF16),
        pltpu.VMEM((4, 32, 256), BF16),
        pltpu.VMEM((4, 4, 4, 32, 256), BF16),
        pltpu.VMEM((3, 512, 256), F32),
        [s for _, size in ROW_PARTS for s in part_shapes(size, 512)],
        pltpu.SemaphoreType.DMA((COPIES,)),
        pltpu.SemaphoreType.DMA((COPIES,)),
        pltpu.SemaphoreType.DMA((LOADS,)),
    ]
    high, grad = pl.pallas_call(
        kernel,
        out_shape=(
            jax.ShapeDtypeStruct((4, 32, 512), BF16),
            jax.ShapeDtypeStruct((3, 512, 256), F32),
        ),
        in_specs=[far] * 5 + [scalars] * 2 + [far] * 6,
        out_specs=(anywhere, anywhere),
        scratch_shapes=scratch,
        compiler_params=pltpu.CompilerParams(
            collective_id=0, has_side_effects=True, vmem_limit_bytes=60 * 2**20
        ),
        name="verify_join",
    )(
        queries, keys_new, values_new, cache_keys.reshape(4, 512, 128), cache_values.reshape(4, 512, 128),
        cache_len, accepted, entering, low_feature.reshape(4, 32, 512), mid_feature.reshape(4, 32, 512),
        out_proj, join_weight.reshape(1536, 256), teacher,
    )
    high, grad = pl.pallas_call(
        deliver,
        out_shape=(
            jax.ShapeDtypeStruct((4, 32, 512), BF16),
            jax.ShapeDtypeStruct((3, 512, 256), F32),
        ),
        in_specs=[anywhere] * 2,
        out_specs=(anywhere, anywhere),
        scratch_shapes=[
            pltpu.VMEM((4, 32, 512), BF16),
            pltpu.VMEM((3, 512, 256), F32),
            pltpu.SemaphoreType.DMA((2, 4)),
        ],
        compiler_params=pltpu.CompilerParams(vmem_limit_bytes=60 * 2**20),
        name="deliver",
    )(high, grad)
    return high.reshape(128, 512), grad


def solution(mesh):
    return jax.shard_map(
        shards,
        mesh=mesh,
        in_specs=(
            P("group", "tensor"),
            P("group", "tensor"),
            P("group", "tensor"),
            P("group", "tensor", None, None),
            P("group", "tensor", None, None),
            P("group"),
            P("group"),
            P("group", "tensor"),
            P("group", "tensor"),
            P("group", "tensor"),
            P("tensor", None),
            P(None, "tensor", "group"),
            P("group", None),
        ),
        out_specs=(P("group", "tensor"), P(None, "tensor", "group")),
        check_vma=False,
    )
```
